256 devices in a mesh: tile: 64 (over z, y, core), tm: 4 (over x).
Axes of the slice: x: 4, y: 4, z: 8, core: 2. Of those that a mesh axis runs over, the one named last changes fastest.
Arguments:
- latent: bfloat16 [12, 192, 1024], P('tm', 'tile'), may hold values from -56 to 56
- conv_in_weight: bfloat16 [3, 3, 3, 16, 384], replicated, may hold values from -0.3125 to 0.3125
- conv_in_bias: float32 [384], replicated, may hold values from -3 to 3
- first_gain: float32 [384], replicated, may hold values from 0.25 to 1.75
- conv_weight: bfloat16 [3, 3, 3, 384, 384], replicated, may hold values from -0.0625 to 0.0625
- conv_bias: float32 [384], replicated, may hold values from -3 to 3
- up_weight: bfloat16 [3, 3, 384, 192], replicated, may hold values from -0.109375 to 0.109375
- up_bias: float32 [192], replicated, may hold values from -3 to 3
Outputs:
- upsampled: bfloat16 [12, 64, 16, 48, 192], P('tm', 'tile')
The draws below stay inside these ranges and needn't reach their ends.
All inputs are finite; a program needn't handle non-finite values.
Results may differ from the reference program's by a relative error of at most 0.0065.
Values may be sent and summed in bfloat16 or wider, within the bound.
No kernel may reach another device: no remote copies, remote signals or barrier semaphores. Data moves between devices by JAX's collectives and lax.ppermute only.
A program may use at most 64 MiB of HBM per device.

```python
import math
from functools import partial
import jax
import jax.numpy as jnp
from jax import lax

LAT_C = 16
C = 384
C_UP = 192
HL = 8
WL = 24
GRID_COLS = 8
GRID_ROWS = 8
F = 12
N_TILE = 64


def draw_latent(key, part):
    key = jax.random.fold_in(key, 17)
    noise_key, cell_key, chan_key = jax.random.split(key, 3)
    cells = HL * WL
    base = jnp.clip(jax.random.normal(noise_key, (F, cells, N_TILE, LAT_C), jnp.float32), -4.0, 4.0)
    spread = math.log(10.0)
    cell_scale = jnp.exp(jax.random.uniform(cell_key, (1, cells, N_TILE, 1), jnp.float32, 0.0, 0.5 * spread))
    chan_scale = jnp.exp(jax.random.uniform(chan_key, (1, 1, 1, LAT_C), jnp.float32, 0.0, 0.5 * spread))
    values = base * cell_scale * chan_scale
    return values.reshape(F, cells, N_TILE * LAT_C).astype(jnp.bfloat16)


def gaussian(own_key, shape, width, limit, dtype=jnp.bfloat16):
    values = jax.random.normal(own_key, shape, jnp.float32) * width
    return jnp.minimum(jnp.maximum(values, -limit), limit).astype(dtype)


def setup_inputs(seed: int = 0) -> dict:
    keys = jax.random.split(jax.random.key(seed), 9)
    return {
        "latent": draw_latent(jax.random.fold_in(keys[8], 71), 0),
        "conv_in_weight": gaussian(keys[1], (3, 3, 3, LAT_C, C), (27 * LAT_C) ** -0.5, 0.3125),
        "conv_in_bias": gaussian(keys[2], (C,), 0.5, 3.0, jnp.float32),
        "first_gain": jnp.clip(1.0 + 0.15 * jax.random.normal(keys[3], (C,), jnp.float32), 0.25, 1.75),
        "conv_weight": gaussian(keys[4], (3, 3, 3, C, C), (27 * C) ** -0.5, 0.0625),
        "conv_bias": gaussian(keys[5], (C,), 0.5, 3.0, jnp.float32),
        "up_weight": gaussian(keys[6], (3, 3, C, C_UP), (9 * C) ** -0.5, 0.109375),
        "up_bias": gaussian(keys[7], (C_UP,), 0.5, 3.0, jnp.float32),
    }


def causal_conv(field, weight):
    padded = jnp.pad(field.astype(jnp.float32), ((2, 0), (1, 1), (1, 1), (0, 0)))
    return lax.conv_general_dilated(padded[None], weight.astype(jnp.float32), (1, 1, 1), 'VALID', dimension_numbers=('NDHWC', 'DHWIO', 'NDHWC'), precision=lax.Precision.HIGHEST)[0]

def activate(field, gain_vector):
    values = field.astype(jnp.float32)
    scaling = lax.rsqrt(lax.optimization_barrier(jnp.mean(values * values, axis=-1, keepdims=True)) + 1e-06)
    return jax.nn.silu(values * scaling * gain_vector).astype(jnp.bfloat16)

def up_picture(picture, up_weight):
    doubled = jnp.repeat(jnp.repeat(picture.astype(jnp.float32), 2, axis=0), 2, axis=1)
    padded = jnp.pad(doubled, ((1, 1), (1, 1), (0, 0)))
    return lax.conv_general_dilated(padded[None], up_weight.astype(jnp.float32), (1, 1), 'VALID', dimension_numbers=('NHWC', 'HWIO', 'NHWC'), precision=lax.Precision.HIGHEST)[0]

def reference(latent, conv_in_weight, conv_in_bias, first_gain, conv_weight, conv_bias, up_weight, up_bias):
    grid = latent.reshape(F, HL, WL, GRID_ROWS, GRID_COLS, LAT_C).transpose(0, 3, 1, 4, 2, 5)
    grid = grid.reshape(F, GRID_ROWS * HL, GRID_COLS * WL, LAT_C)
    start = (causal_conv(grid, conv_in_weight) + conv_in_bias).astype(jnp.bfloat16)
    active = activate(start, first_gain)
    hidden = (start.astype(jnp.float32) + causal_conv(active, conv_weight) + conv_bias).astype(jnp.bfloat16)
    result = lax.map(partial(up_picture, up_weight=up_weight), hidden) + up_bias
    result = result.astype(jnp.bfloat16)
    result = result.reshape(F, GRID_ROWS, 2 * HL, GRID_COLS, 2 * WL, C_UP).transpose(0, 1, 3, 2, 4, 5)
    return result.reshape(F, N_TILE, 2 * HL, 2 * WL, C_UP)
```

```python
import jax
import jax.numpy as jnp
from jax import lax
from jax.experimental import pallas as pl
from jax.experimental.pallas import tpu as pltpu
from jax.sharding import PartitionSpec as P

LAT_C = 16
C = 384
C_UP = 192
HL = 8
WL = 24
GRID = 8
S = 32
LANE_OF_FRAME = (48, 0, 16, 32, 64, 80, 96)


def exchange(latent):
    tiles = latent.reshape(3, 3, GRID, GRID, LAT_C).transpose(2, 3, 1, 0, 4)
    tiles = jnp.concatenate([tiles, tiles[:, :, :, 2:]], axis=3).reshape(GRID, GRID, 3 * 64)
    index = lax.axis_index("tile")
    r, g = index // GRID, index % GRID
    side = jnp.where(g < 4, jnp.roll(tiles, -1, axis=1), jnp.roll(tiles, 1, axis=1))
    wide = jnp.concatenate([tiles, side], axis=2)
    other = jnp.where(r < 4, jnp.roll(wide, -1, axis=0), jnp.roll(wide, 1, axis=0))
    pieces = jnp.stack([wide, other], axis=2).reshape(1, GRID * GRID, 2, 6 * 64)
    count = lax.axis_size("tm")
    send = jnp.broadcast_to(pieces, (count, GRID * GRID, 2, 6 * 64)).reshape(count * GRID * GRID, 2, 6 * 64)
    moved = lax.all_to_all(send, ("tm", "tile"), split_axis=0, concat_axis=0, tiled=True)
    return moved.reshape(count * GRID * GRID * 2, 6 * 64)


def prepare(w1_ref, w2_ref, up_ref, t1_ref, t2_ref, tu_ref, sem):
    copies = [
        pltpu.make_async_copy(w2_ref.at[dt], t2_ref.at[:, (2 - dt) * C : (3 - dt) * C], sem.at[dt])
        for dt in range(3)
    ]
    for copy in copies:
        copy.start()
    t1_ref[...] = jnp.zeros(t1_ref.shape, t1_ref.dtype)
    for tap in range(9):
        for frame in range(5):
            for dt in range(3):
                row = tap * 128 + LANE_OF_FRAME[frame + dt]
                source = (dt * 9 + tap) * LAT_C
                t1_ref[row : row + LAT_C, frame * C : (frame + 1) * C] = w1_ref[source : source + LAT_C, :]
    tu_ref[...] = jnp.zeros(tu_ref.shape, tu_ref.dtype)
    groups = (((0,), (1, 2)), ((0, 1), (2,)))
    for py in range(2):
        for px in range(2):
            for ey in range(2):
                for ex in range(2):
                    total = None
                    for dy in groups[py][ey]:
                        for dx in groups[px][ex]:
                            part = up_ref[dy * 3 + dx].astype(jnp.float32)
                            total = part if total is None else total + part
                    row = (ey * 2 + ex) * C
                    tu_ref[py * 2 + px, row : row + C, 0:C_UP] = total.T.astype(jnp.bfloat16)
    for copy in copies:
        copy.wait()


def place(shape, dim):
    return lax.broadcasted_iota(jnp.int32, shape, dim)


def section(
    recv_ref, t1_ref, t2_ref, tu_ref, b1_ref, gain_ref, b2_ref, bu_ref, out_ref,
    x_ref, l1_ref, act_ref, la_ref, acc_ref, lh_ref, up_ref,
):
    x = lax.axis_index("tm")
    tile = lax.axis_index("tile")
    a, b = lax.div(tile, GRID), lax.rem(tile, GRID)
    f32, bf16 = jnp.float32, jnp.bfloat16

    blocks = []
    for d in range(3):
        first = pl.multiple_of(jnp.maximum(x - d, 0) * 128, 128)
        block = recv_ref[pl.ds(first, 128), :].astype(f32)
        blocks.append(jnp.where(x >= d, block, 0.0))
    lane = place((128, 128), 1)
    parts = []
    for j in range(3):
        now, before, older = [block[:, j * 128 : (j + 1) * 128] for block in blocks]
        past = jnp.where((lane & 63) >= 48, older, before)
        parts.append(jnp.where(lane < 64, past, pltpu.roll(now, 64, 1)))
        parts.append(jnp.where(lane < 64, pltpu.roll(past, 64, 1), now))
    rows = 14 * S
    stacked = jnp.concatenate(
        [parts[h * 3 + cell].astype(bf16) for cell in range(3) for h in range(2)], axis=0
    )
    row = place((rows, 768), 0)
    big_r, col = row >> 5, row & 31
    group = (col * 43) >> 7
    cell = col - 3 * group
    r = (big_r + 5) & 7
    g = (group + 7) & 7
    outer_r = jnp.where((big_r < 3) | (big_r >= 11), 1, 0)
    outer_g = jnp.where((group == 0) | (group == 9), 1, 0)
    source = cell * 256 + outer_g * 128 + r * 16 + g * 2 + outer_r
    frame_r = big_r + a * 8 - 3
    frame_c = col + b * 24 - 3
    inside = (frame_r >= 0) & (frame_r < 64) & (frame_c >= 0) & (frame_c < 192) & (col < 30)
    pick = jnp.where((place((rows, 768), 1) == source) & inside, 1.0, 0.0).astype(bf16)
    x_ref[0:rows, :] = jnp.dot(pick, stacked, preferred_element_type=f32)
    x_ref[rows : rows + 8, :] = jnp.zeros((8, 128), f32)
    for dx in range(3):
        l1_ref[:, dx * 128 : (dx + 1) * 128] = x_ref[pl.ds(dx, rows), :].astype(bf16)

    m1 = 12 * S
    lhs = jnp.concatenate([l1_ref[dy * S : dy * S + m1, :] for dy in range(3)], axis=1)
    position = place((m1, 1), 0)
    frame_r = (position >> 5) + a * 8 - 2
    frame_c = (position & 31) + b * 24 - 2
    inside = (frame_r >= 0) & (frame_r < 64) & (frame_c >= 0) & (frame_c < 192)
    m2 = 10 * S
    act_ref[m1 : m1 + 8, :] = jnp.zeros((8, C), f32)
    for frame in range(5):
        field = jnp.dot(lhs, t1_ref[:, frame * C : (frame + 1) * C], preferred_element_type=f32) + b1_ref[...]
        start = field.astype(bf16).astype(f32)
        if frame >= 2:
            act_ref[0:m1, :] = start
            acc_ref[:, (frame - 2) * C : (frame - 1) * C] = act_ref[pl.ds(S + 1, m2), :] + b2_ref[...]
        scaling = lax.rsqrt(jnp.mean(start * start, axis=1, keepdims=True) + 1e-06)
        value = start * scaling * gain_ref[...]
        value = value / (1.0 + jnp.exp(-value))
        keep = inside if frame >= 2 else inside & (x > 0)
        act_ref[0:m1, :] = jnp.where(keep, value, 0.0)
        for dx in range(3):
            la_ref[frame, :, dx * C : (dx + 1) * C] = act_ref[pl.ds(dx, m1), :].astype(bf16)

    for frame in range(5):
        lhs = jnp.concatenate([la_ref[frame, dy * S : dy * S + m2, :] for dy in range(3)], axis=1)
        low, high = max(0, frame - 2), min(2, frame)
        for t in range(low, high + 1):
            block = 2 - frame + t
            acc_ref[:, t * C : (t + 1) * C] += jnp.dot(
                lhs, t2_ref[:, block * C : (block + 1) * C], preferred_element_type=f32
            )

    position = place((m2, 1), 0)
    frame_r = (position >> 5) + a * 8 - 1
    frame_c = (position & 31) + b * 24 - 1
    inside = (frame_r >= 0) & (frame_r < 64) & (frame_c >= 0) & (frame_c < 192)
    m3 = 8 * S
    for t in range(3):
        act_ref[0:m2, :] = jnp.where(inside, acc_ref[:, t * C : (t + 1) * C], 0.0)
        for dx in range(3):
            lh_ref[:, dx * C : (dx + 1) * C] = act_ref[pl.ds(dx, m2), :].astype(bf16)
        for py in range(2):
            for px in range(2):
                lhs = jnp.concatenate(
                    [
                        lh_ref[(py + ey) * S : (py + ey) * S + m3, (px + ex) * C : (px + ex + 1) * C]
                        for ey in range(2)
                        for ex in range(2)
                    ],
                    axis=1,
                )
                phase = jnp.dot(lhs, tu_ref[py * 2 + px], preferred_element_type=f32) + bu_ref[...]
                for y in range(HL):
                    for part in range(2):
                        up_ref[part, 2 * y + py, pl.ds(px, WL, stride=2), :] = phase[
                            y * S : y * S + WL, part * 128 : (part + 1) * 128
                        ]
        out_ref[t, 0, :, :, 0:128] = up_ref[0].astype(bf16)
        out_ref[t, 0, :, :, 128:C_UP] = up_ref[1, :, :, 0 : C_UP - 128].astype(bf16)


def on_device(
    latent, conv_in_weight, conv_in_bias, first_gain, conv_weight, conv_bias, up_weight, up_bias
):
    vmem = pl.BlockSpec(memory_space=pltpu.VMEM)
    bf16, f32 = jnp.bfloat16, jnp.float32
    prepared = pl.pallas_call(
        prepare,
        out_shape=[
            pltpu.VMEM((9 * 128, 5 * C), bf16),
            pltpu.VMEM((9 * C, 3 * C), bf16),
            pltpu.VMEM((4, 4 * C, 256), bf16),
        ],
        in_specs=[vmem, pl.BlockSpec(memory_space=pl.ANY), vmem],
        out_specs=[vmem, vmem, vmem],
        scratch_shapes=[pltpu.SemaphoreType.DMA((3,))],
        compiler_params=pltpu.CompilerParams(vmem_limit_bytes=28 * 2**20),
        cost_estimate=pl.CostEstimate(flops=10**9, bytes_accessed=20_000_000, transcendentals=0),
        name="prepare",
    )(
        conv_in_weight.reshape(27 * LAT_C, C),
        conv_weight.reshape(3, 9 * C, C),
        up_weight.transpose(0, 1, 3, 2).reshape(9, C_UP, C),
    )
    received = exchange(latent)
    return pl.pallas_call(
        section,
        out_shape=jax.ShapeDtypeStruct((3, 1, 2 * HL, 2 * WL, C_UP), bf16),
        in_specs=[vmem] * 8,
        out_specs=vmem,
        scratch_shapes=[
            pltpu.VMEM((14 * S + 8, 128), f32),
            pltpu.VMEM((14 * S, 3 * 128), bf16),
            pltpu.VMEM((12 * S + 8, C), f32),
            pltpu.VMEM((5, 12 * S, 3 * C), bf16),
            pltpu.VMEM((10 * S, 3 * C), f32),
            pltpu.VMEM((10 * S, 3 * C), bf16),
            pltpu.VMEM((2, 2 * HL, 2 * WL, 128), f32),
        ],
        compiler_params=pltpu.CompilerParams(vmem_limit_bytes=36 * 2**20),
        cost_estimate=pl.CostEstimate(flops=8 * 10**9, bytes_accessed=2_000_000, transcendentals=10**6),
        name="section",
    )(
        received,
        *prepared,
        conv_in_bias.reshape(1, C),
        first_gain.reshape(1, C),
        conv_bias.reshape(1, C),
        jnp.pad(up_bias, (0, 256 - C_UP)).reshape(1, 256),
    )


def solution(mesh):
    return jax.shard_map(
        on_device,
        mesh=mesh,
        in_specs=(P("tm", "tile", None), P(), P(), P(), P(), P(), P(), P()),
        out_specs=P("tm", "tile", None, None, None),
        check_vma=False,
    )
```

```python
import jax
import jax.numpy as jnp
from jax import lax
from jax.experimental import pallas as pl
from jax.experimental.pallas import tpu as pltpu
from jax.sharding import PartitionSpec as P

LAT_C = 16
C = 384
C_UP = 192
HL = 8
WL = 24
GRID = 8
S = 32
M0, M1, M2, M3 = 14 * S, 12 * S, 10 * S, 8 * S
bf16, f32 = jnp.bfloat16, jnp.float32
VMEM = pl.BlockSpec(memory_space=pltpu.VMEM)
HBM = pl.BlockSpec(memory_space=pltpu.HBM)


def gather(latent):
    tiles = latent.reshape(3, 3, GRID, GRID, LAT_C).transpose(2, 3, 1, 0, 4)
    tiles = jnp.concatenate([tiles, tiles[:, :, :, 2:]], axis=3).reshape(GRID, GRID, 3 * 64)
    index = lax.axis_index("tile")
    r, g = index // GRID, index % GRID
    side = jnp.where(g < 4, jnp.roll(tiles, -1, axis=1), jnp.roll(tiles, 1, axis=1))
    wide = jnp.concatenate([tiles, side], axis=2)
    other = jnp.where(r < 4, jnp.roll(wide, -1, axis=0), jnp.roll(wide, 1, axis=0))
    pieces = jnp.stack([wide, other], axis=2).reshape(GRID * GRID, 2, 6 * 64)
    own = lax.all_to_all(pieces, "tile", split_axis=0, concat_axis=0, tiled=True)
    return own.reshape(GRID * GRID * 2, 6 * 64)


def place(shape, dim):
    return lax.broadcasted_iota(jnp.int32, shape, dim)


def origin():
    tile = lax.axis_index("tile")
    return lax.div(tile, GRID), lax.rem(tile, GRID)


def inside(rows, margin):
    a, b = origin()
    position = place((rows, 1), 0)
    row = (position >> 5) + a * HL - margin
    column = (position & 31) + b * WL - margin
    return (row >= 0) & (row < GRID * HL) & (column >= 0) & (column < GRID * WL)


def assemble(pieces_ref, own_ref, last_ref):
    a, b = origin()
    parts = []
    for j in range(3):
        group = pieces_ref[:, j * 128 : (j + 1) * 128].astype(f32)
        parts += [group, pltpu.roll(group, 64, 1)]
    stacked = jnp.concatenate(
        [parts[h * 3 + cell].astype(bf16) for cell in range(3) for h in range(2)], axis=0
    )
    row = place((M0, 1), 0)
    big_r, col = row >> 5, row & 31
    group = (col * 43) >> 7
    cell = col - 3 * group
    r = (big_r + 5) & 7
    g = (group + 7) & 7
    outer_r = jnp.where((big_r < 3) | (big_r >= 11), 1, 0)
    outer_g = jnp.where((group == 0) | (group == 9), 1, 0)
    source = cell * 256 + outer_g * 128 + r * 16 + g * 2 + outer_r
    source = jnp.where(inside(M0, 3) & (col < 30), source, -1)
    pick = jnp.where(place((M0, 768), 1) == source, 1.0, 0.0).astype(bf16)
    field = jnp.dot(pick, stacked, preferred_element_type=f32)
    half = M0 // 2
    lane = place((half, 128), 1)
    own_ref[...] = jnp.where(lane < 64, field[:half], pltpu.roll(field[half:], 64, 1)).astype(bf16)
    part = M0 // 8
    lane = place((part, 128), 1) >> 4
    last = jnp.zeros((part, 128), f32)
    for i in range(8):
        shift = (16 * i - 32) % 128
        rows = field[i * part : (i + 1) * part]
        last = jnp.where(lane == i, pltpu.roll(rows, shift, 1) if shift else rows, last)
    last_ref[...] = last.astype(bf16)


def side_by_side(x_ref, shift, target):
    low = place((M0, 128), 1) < 64
    left, middle, right = [
        pltpu.roll(x_ref[pl.ds(dx, M0), :], (64 * (dx % 2) + shift) % 128, 1) for dx in range(3)
    ]
    target[:, 0:128] = jnp.where(low, left, middle).astype(bf16)
    target[:, 128:256] = right.astype(bf16)


def taps(w1_ref, t1_ref, frames):
    t1_ref[...] = jnp.zeros(t1_ref.shape, t1_ref.dtype)
    for tap in range(9):
        for dt in range(3):
            for frame in range(frames):
                row = (tap // 3) * 256 + (tap % 3) * 64 + (frame + dt) * LAT_C
                source = (dt * 9 + tap) * LAT_C
                t1_ref[row : row + LAT_C, frame * C : (frame + 1) * C] = w1_ref[source : source + LAT_C, :]


def rows_of(ref, height):
    return jnp.concatenate([ref[dy * S : dy * S + height, :] for dy in range(3)], axis=1)


def spread(field_ref, height, target):
    for dx in range(3):
        target[:, dx * C : (dx + 1) * C] = field_ref[pl.ds(dx, height), :].astype(bf16)


def activate(start, gain, keep, act_ref, target):
    scaling = lax.rsqrt(jnp.mean(start * start, axis=1, keepdims=True) + 1e-06)
    value = start * scaling * gain
    value = value / (1.0 + jnp.exp(-value))
    act_ref[0:M1, :] = jnp.where(keep, value, 0.0)
    act_ref[M1 : M1 + 8, :] = jnp.zeros((8, C), f32)
    spread(act_ref, M1, target)


def front(
    own_ref, w1_ref, up_ref, w2_hbm, b1_ref, gain_ref, b2_ref, acc_ref, tu_ref, w2_ref,
    t1_ref, sem, x_ref, l1_ref, act_ref, la_ref,
):
    loads = [pltpu.make_async_copy(w2_hbm.at[dt], w2_ref.at[dt], sem.at[dt]) for dt in (2, 0, 1)]
    for load in loads:
        load.start()
    b1, gain, b2 = [ref[...].reshape(1, C) for ref in (b1_ref, gain_ref, b2_ref)]
    taps(w1_ref, t1_ref, 1)
    half = M0 // 2
    packed = own_ref[...].astype(f32)
    x_ref[0:half, :] = packed
    x_ref[half:M0, :] = pltpu.roll(packed, 64, 1)
    x_ref[M0 : M0 + 8, :] = jnp.zeros((8, 128), f32)
    side_by_side(x_ref, 0, l1_ref)
    field = jnp.dot(rows_of(l1_ref, M1), t1_ref[...], preferred_element_type=f32) + b1
    start = field.astype(bf16).astype(f32)
    act_ref[0:M1, :] = start
    residual = act_ref[pl.ds(S + 1, M2), :] + b2
    activate(start, gain, inside(M1, 2), act_ref, la_ref)
    groups = (((0,), (1, 2)), ((0, 1), (2,)))
    for py in range(2):
        for px in range(2):
            for ey in range(2):
                for ex in range(2):
                    total = None
                    for dy in groups[py][ey]:
                        for dx in groups[px][ex]:
                            part = up_ref[dy * 3 + dx].astype(f32)
                            total = part if total is None else total + part
                    row = (ey * 2 + ex) * C
                    tu_ref[py * 2 + px, row : row + C, 0:C_UP] = total.T.astype(bf16)
            tu_ref[py * 2 + px, :, C_UP:256] = jnp.zeros((4 * C, 256 - C_UP), bf16)
    loads[0].wait()
    acc_ref[...] = residual + jnp.dot(rows_of(la_ref, M2), w2_ref[2], preferred_element_type=f32)
    for load in loads[1:]:
        load.wait()


def back(
    own_ref, before_ref, older_ref, acc4_ref, w1_ref, tu_ref, w2_ref, b1_ref, gain_ref, b2_ref, bu_ref, out_hbm,
    t1_ref, sem, x_ref, l1_ref, act_ref, la_ref, acc_ref, lh_ref, up_ref, out_ref,
):
    b1, gain, b2 = [ref[...].reshape(1, C) for ref in (b1_ref, gain_ref, b2_ref)]
    bu = jnp.concatenate([bu_ref[...].reshape(1, C_UP), jnp.zeros((1, 256 - C_UP), f32)], axis=1)

    half, part = M0 // 2, M0 // 8
    now, before, older = [ref[...].astype(f32) for ref in (own_ref, before_ref, older_ref)]
    lane = place((half, 128), 1)
    for i in range(2):
        past = pltpu.roll(before, 64, 1) if i else before
        old = jnp.concatenate([pltpu.roll(older, 112 - 16 * (4 * i + k), 1) if 4 * i + k < 7 else older for k in range(4)], axis=0)
        x_ref[i * half : (i + 1) * half, :] = jnp.where(
            lane < 48, past, jnp.where(lane < 96, pltpu.roll(now, 112 if i else 48, 1), old)
        )
    x_ref[M0 : M0 + 8, :] = jnp.zeros((8, 128), f32)
    taps(w1_ref, t1_ref, 2)

    keep = inside(M1, 2)
    x = lax.axis_index("tm")
    for pair in range(2):
        side_by_side(x_ref, (16 - 32 * pair) % 128, l1_ref.at[pair])
        fields = jnp.dot(rows_of(l1_ref.at[pair], M1), t1_ref[...], preferred_element_type=f32)
        for k in range(2):
            frame = 2 * pair + k
            start = (fields[:, k * C : (k + 1) * C] + b1).astype(bf16).astype(f32)
            act = act_ref.at[frame]
            if pair:
                act[0:M1, :] = start
                acc_ref[:, k * C : (k + 1) * C] = act[pl.ds(S + 1, M2), :] + b2
            activate(start, gain, keep if pair else keep & (x > 0), act, la_ref.at[frame])
    acc_ref[:, 2 * C : 3 * C] = acc4_ref[...]

    for frame in range(4):
        low, high = max(0, frame - 2), min(2, frame)
        weight = jnp.concatenate([w2_ref[frame - t] for t in range(low, high + 1)], axis=1)
        acc_ref[:, low * C : (high + 1) * C] += jnp.dot(
            rows_of(la_ref.at[frame], M2), weight, preferred_element_type=f32
        )

    keep = inside(M2, 1)
    for t in range(3):
        act_ref[t, 0:M2, :] = jnp.where(keep, acc_ref[:, t * C : (t + 1) * C], 0.0)
        spread(act_ref.at[t], M2, lh_ref.at[t])
    for py in range(2):
        for px in range(2):
            lhs = jnp.concatenate(
                [
                    jnp.concatenate(
                        [
                            lh_ref[t, (py + ey) * S : (py + ey) * S + M3, (px + ex) * C : (px + ex + 1) * C]
                            for t in range(3)
                        ],
                        axis=0,
                    )
                    for ey in range(2)
                    for ex in range(2)
                ],
                axis=1,
            )
            phase = jnp.dot(lhs, tu_ref[py * 2 + px], preferred_element_type=f32) + bu
            for t in range(3):
                for y in range(HL):
                    row = t * M3 + y * S
                    for side in range(2):
                        up_ref[t, side, 2 * y + py, pl.ds(px, WL, stride=2), :] = phase[
                            row : row + WL, side * 128 : (side + 1) * 128
                        ]
    stores = []
    for t in range(3):
        out_ref[t, 0, :, :, 0:128] = up_ref[t, 0].astype(bf16)
        out_ref[t, 0, :, :, 128:C_UP] = up_ref[t, 1, :, :, 0 : C_UP - 128].astype(bf16)
        stores.append(pltpu.make_async_copy(out_ref.at[t], out_hbm.at[t], sem.at[t]))
        stores[-1].start()
    for store in stores:
        store.wait()


def on_device(
    latent, conv_in_weight, conv_in_bias, first_gain, conv_weight, conv_bias, up_weight, up_bias
):
    w1 = conv_in_weight.reshape(27 * LAT_C, C)
    w2 = pltpu.with_memory_space_constraint(conv_weight.reshape(3, 9 * C, C), pltpu.HBM)
    own, last = pl.pallas_call(
        assemble,
        out_shape=[jax.ShapeDtypeStruct((M0 // 2, 128), bf16), jax.ShapeDtypeStruct((M0 // 8, 128), bf16)],
        in_specs=[VMEM],
        out_specs=[VMEM, VMEM],
        compiler_params=pltpu.CompilerParams(vmem_limit_bytes=8 * 2**20),
        cost_estimate=pl.CostEstimate(flops=10**8, bytes_accessed=10**6, transcendentals=0),
        name="assemble",
    )(gather(latent))
    count = lax.axis_size("tm")
    before = lax.ppermute(own, "tm", [(i, i + 1) for i in range(count - 1)])
    older = lax.ppermute(last, "tm", [(i, i + 2) for i in range(count - 2)])
    acc4, tu, w2 = pl.pallas_call(
        front,
        out_shape=[
            jax.ShapeDtypeStruct((M2, C), f32),
            jax.ShapeDtypeStruct((4, 4 * C, 256), bf16),
            pltpu.VMEM((3, 9 * C, C), bf16),
        ],
        in_specs=[VMEM, VMEM, VMEM, HBM, VMEM, VMEM, VMEM],
        out_specs=[VMEM, VMEM, VMEM],
        scratch_shapes=[
            pltpu.VMEM((3 * 256, C), bf16),
            pltpu.SemaphoreType.DMA((3,)),
            pltpu.VMEM((M0 + 8, 128), f32),
            pltpu.VMEM((M0, 256), bf16),
            pltpu.VMEM((M1 + 8, C), f32),
            pltpu.VMEM((M1, 3 * C), bf16),
        ],
        compiler_params=pltpu.CompilerParams(vmem_limit_bytes=24 * 2**20),
        cost_estimate=pl.CostEstimate(flops=10**9, bytes_accessed=10_000_000, transcendentals=10**6),
        name="front",
    )(own, w1, up_weight.transpose(0, 1, 3, 2).reshape(9, C_UP, C), w2, conv_in_bias, first_gain, conv_bias)
    return pl.pallas_call(
        back,
        out_shape=jax.ShapeDtypeStruct((3, 1, 2 * HL, 2 * WL, C_UP), bf16),
        in_specs=[VMEM] * 11,
        out_specs=HBM,
        scratch_shapes=[
            pltpu.VMEM((3 * 256, 2 * C), bf16),
            pltpu.SemaphoreType.DMA((3,)),
            pltpu.VMEM((M0 + 8, 128), f32),
            pltpu.VMEM((2, M0, 256), bf16),
            pltpu.VMEM((4, M1 + 8, C), f32),
            pltpu.VMEM((4, M1, 3 * C), bf16),
            pltpu.VMEM((M2, 3 * C), f32),
            pltpu.VMEM((3, M2, 3 * C), bf16),
            pltpu.VMEM((3, 2, 2 * HL, 2 * WL, 128), f32),
            pltpu.VMEM((3, 1, 2 * HL, 2 * WL, C_UP), bf16),
        ],
        compiler_params=pltpu.CompilerParams(vmem_limit_bytes=32 * 2**20),
        cost_estimate=pl.CostEstimate(flops=8 * 10**9, bytes_accessed=12_000_000, transcendentals=10**6),
        name="back",
    )(own, before, older, acc4, w1, tu, w2, conv_in_bias, first_gain, conv_bias, up_bias)


def solution(mesh):
    return jax.shard_map(
        on_device,
        mesh=mesh,
        in_specs=(P("tm", "tile", None), P(), P(), P(), P(), P(), P(), P()),
        out_specs=P("tm", "tile", None, None, None),
        check_vma=False,
    )
```

```python
import jax
import jax.numpy as jnp
from jax import lax
from jax.experimental import pallas as pl
from jax.experimental.pallas import tpu as pltpu
from jax.sharding import PartitionSpec as P

LAT_C = 16
C = 384
C_UP = 192
HL = 8
WL = 24
GRID = 8
S = 32
M0, M1, M2, M3 = 14 * S, 12 * S, 10 * S, 8 * S
bf16, f32 = jnp.bfloat16, jnp.float32
VMEM = pl.BlockSpec(memory_space=pltpu.VMEM)
HBM = pl.BlockSpec(memory_space=pltpu.HBM)


def gather(latent):
    tiles = latent.reshape(3, 3, GRID, GRID, LAT_C).transpose(2, 3, 1, 0, 4)
    tiles = jnp.concatenate([tiles, tiles[:, :, :, 2:]], axis=3).reshape(GRID, GRID, 3 * 64)
    index = lax.axis_index("tile")
    r, g = index // GRID, index % GRID
    side = jnp.where(g < 4, jnp.roll(tiles, -1, axis=1), jnp.roll(tiles, 1, axis=1))
    wide = jnp.concatenate([tiles, side], axis=2)
    other = jnp.where(r < 4, jnp.roll(wide, -1, axis=0), jnp.roll(wide, 1, axis=0))
    pieces = jnp.stack([wide, other], axis=2).reshape(GRID * GRID, 2, 6 * 64)
    own = lax.all_to_all(pieces, "tile", split_axis=0, concat_axis=0, tiled=True)
    return own.reshape(GRID * GRID * 2, 6 * 64)


def place(shape, dim):
    return lax.broadcasted_iota(jnp.int32, shape, dim)


def origin():
    tile = lax.axis_index("tile")
    return lax.div(tile, GRID), lax.rem(tile, GRID)


def inside(rows, margin):
    a, b = origin()
    position = place((rows, 1), 0)
    row = (position >> 5) + a * HL - margin
    column = (position & 31) + b * WL - margin
    return (row >= 0) & (row < GRID * HL) & (column >= 0) & (column < GRID * WL)


def assemble(pieces_ref, own_ref, last_ref):
    a, b = origin()
    parts = []
    for j in range(3):
        group = pieces_ref[:, j * 128 : (j + 1) * 128].astype(f32)
        parts += [group, pltpu.roll(group, 64, 1)]
    stacked = jnp.concatenate(
        [parts[h * 3 + cell].astype(bf16) for cell in range(3) for h in range(2)], axis=0
    )
    row = place((M0, 1), 0)
    big_r, col = row >> 5, row & 31
    group = (col * 43) >> 7
    cell = col - 3 * group
    r = (big_r + 5) & 7
    g = (group + 7) & 7
    outer_r = jnp.where((big_r < 3) | (big_r >= 11), 1, 0)
    outer_g = jnp.where((group == 0) | (group == 9), 1, 0)
    source = cell * 256 + outer_g * 128 + r * 16 + g * 2 + outer_r
    source = jnp.where(inside(M0, 3) & (col < 30), source, -1)
    pick = jnp.where(place((M0, 768), 1) == source, 1.0, 0.0).astype(bf16)
    field = jnp.dot(pick, stacked, preferred_element_type=f32)
    half = M0 // 2
    lane = place((half, 128), 1)
    own_ref[...] = jnp.where(lane < 64, field[:half], pltpu.roll(field[half:], 64, 1)).astype(bf16)
    part = M0 // 8
    lane = place((part, 128), 1) >> 4
    last = jnp.zeros((part, 128), f32)
    for i in range(8):
        shift = (16 * i - 32) % 128
        rows = field[i * part : (i + 1) * part]
        last = jnp.where(lane == i, pltpu.roll(rows, shift, 1) if shift else rows, last)
    last_ref[...] = last.astype(bf16)


def side_by_side(x_ref, shift, target):
    low = place((M0, 128), 1) < 64
    left, middle, right = [
        pltpu.roll(x_ref[pl.ds(dx, M0), :], (64 * (dx % 2) + shift) % 128, 1) for dx in range(3)
    ]
    target[:, 0:128] = jnp.where(low, left, middle).astype(bf16)
    target[:, 128:256] = right.astype(bf16)


def taps(w1_ref, t1_ref, frames):
    t1_ref[...] = jnp.zeros(t1_ref.shape, t1_ref.dtype)
    for tap in range(9):
        for dt in range(3):
            for frame in range(frames):
                row = (tap // 3) * 256 + (tap % 3) * 64 + (frame + dt) * LAT_C
                source = (dt * 9 + tap) * LAT_C
                t1_ref[row : row + LAT_C, frame * C : (frame + 1) * C] = w1_ref[source : source + LAT_C, :]


def rows_of(ref, height):
    return jnp.concatenate([ref[dy * S : dy * S + height, :] for dy in range(3)], axis=1)


def spread(field_ref, height, target):
    for dx in range(3):
        target[:, dx * C : (dx + 1) * C] = field_ref[pl.ds(dx, height), :].astype(bf16)


def activate(start, gain, keep, act_ref, target):
    scaling = lax.rsqrt(jnp.mean(start * start, axis=1, keepdims=True) + 1e-06)
    value = start * scaling * gain
    value = value / (1.0 + jnp.exp(-value))
    act_ref[0:M1, :] = jnp.where(keep, value, 0.0)
    act_ref[M1 : M1 + 8, :] = jnp.zeros((8, C), f32)
    spread(act_ref, M1, target)


def front(
    own_ref, w1_ref, up_ref, w2_hbm, b1_ref, gain_ref, b2_ref, acc_ref, tu_ref, w2_ref,
    t1_ref, sem, x_ref, l1_ref, act_ref, la_ref,
):
    loads = [pltpu.make_async_copy(w2_hbm.at[dt], w2_ref.at[dt], sem.at[dt]) for dt in (2, 0, 1)]
    for load in loads:
        load.start()
    b1, gain, b2 = [ref[...].reshape(1, C) for ref in (b1_ref, gain_ref, b2_ref)]
    taps(w1_ref, t1_ref, 1)
    half = M0 // 2
    packed = own_ref[...].astype(f32)
    x_ref[0:half, :] = packed
    x_ref[half:M0, :] = pltpu.roll(packed, 64, 1)
    x_ref[M0 : M0 + 8, :] = jnp.zeros((8, 128), f32)
    side_by_side(x_ref, 0, l1_ref)
    field = jnp.dot(rows_of(l1_ref, M1), t1_ref[...], preferred_element_type=f32) + b1
    start = field.astype(bf16).astype(f32)
    act_ref[0:M1, :] = start
    residual = act_ref[pl.ds(S + 1, M2), :] + b2
    activate(start, gain, inside(M1, 2), act_ref, la_ref)
    groups = (((0,), (1, 2)), ((0, 1), (2,)))
    for py in range(2):
        for px in range(2):
            for ey in range(2):
                for ex in range(2):
                    total = None
                    for dy in groups[py][ey]:
                        for dx in groups[px][ex]:
                            part = up_ref[dy * 3 + dx].astype(f32)
                            total = part if total is None else total + part
                    row = (ey * 2 + ex) * C
                    tu_ref[py * 2 + px, row : row + C, 0:C_UP] = total.T.astype(bf16)
            tu_ref[py * 2 + px, :, C_UP:256] = jnp.zeros((4 * C, 256 - C_UP), bf16)
    loads[0].wait()
    acc_ref[...] = residual + jnp.dot(rows_of(la_ref, M2), w2_ref[2], preferred_element_type=f32)
    for load in loads[1:]:
        load.wait()


def back(
    own_ref, before_ref, older_ref, acc4_ref, w1_ref, tu_ref, w2_ref, b1_ref, gain_ref, b2_ref, bu_ref, out_hbm,
    t1_ref, sem, x_ref, l1_ref, act_ref, la_ref, acc_ref, lh_ref, up_ref, out_ref,
):
    b1, gain, b2 = [ref[...].reshape(1, C) for ref in (b1_ref, gain_ref, b2_ref)]
    bu = jnp.concatenate([bu_ref[...].reshape(1, C_UP), jnp.zeros((1, 256 - C_UP), f32)], axis=1)

    half, part = M0 // 2, M0 // 8
    x = lax.axis_index("tm")
    now, before, older = [
        jnp.where(x >= d, ref[...].astype(f32), 0.0) for d, ref in enumerate((own_ref, before_ref, older_ref))
    ]
    lane = place((half, 128), 1)
    for i in range(2):
        past = pltpu.roll(before, 64, 1) if i else before
        old = jnp.concatenate([pltpu.roll(older, 112 - 16 * (4 * i + k), 1) if 4 * i + k < 7 else older for k in range(4)], axis=0)
        x_ref[i * half : (i + 1) * half, :] = jnp.where(
            lane < 48, past, jnp.where(lane < 96, pltpu.roll(now, 112 if i else 48, 1), old)
        )
    x_ref[M0 : M0 + 8, :] = jnp.zeros((8, 128), f32)
    taps(w1_ref, t1_ref, 2)

    keep = inside(M1, 2)
    for pair in range(2):
        side_by_side(x_ref, (16 - 32 * pair) % 128, l1_ref.at[pair])
        fields = jnp.dot(rows_of(l1_ref.at[pair], M1), t1_ref[...], preferred_element_type=f32)
        for k in range(2):
            frame = 2 * pair + k
            start = (fields[:, k * C : (k + 1) * C] + b1).astype(bf16).astype(f32)
            act = act_ref.at[frame]
            if pair:
                act[0:M1, :] = start
                acc_ref[:, k * C : (k + 1) * C] = act[pl.ds(S + 1, M2), :] + b2
            activate(start, gain, keep if pair else keep & (x > 0), act, la_ref.at[frame])
    acc_ref[:, 2 * C : 3 * C] = acc4_ref[...]

    for frame in range(4):
        low, high = max(0, frame - 2), min(2, frame)
        weight = jnp.concatenate([w2_ref[frame - t] for t in range(low, high + 1)], axis=1)
        acc_ref[:, low * C : (high + 1) * C] += jnp.dot(
            rows_of(la_ref.at[frame], M2), weight, preferred_element_type=f32
        )

    keep = inside(M2, 1)
    for t in range(3):
        act_ref[t, 0:M2, :] = jnp.where(keep, acc_ref[:, t * C : (t + 1) * C], 0.0)
        spread(act_ref.at[t], M2, lh_ref.at[t])
    for py in range(2):
        for px in range(2):
            lhs = jnp.concatenate(
                [
                    jnp.concatenate(
                        [
                            lh_ref[t, (py + ey) * S : (py + ey) * S + M3, (px + ex) * C : (px + ex + 1) * C]
                            for t in range(3)
                        ],
                        axis=0,
                    )
                    for ey in range(2)
                    for ex in range(2)
                ],
                axis=1,
            )
            phase = jnp.dot(lhs, tu_ref[py * 2 + px], preferred_element_type=f32) + bu
            for t in range(3):
                for y in range(HL):
                    row = t * M3 + y * S
                    for side in range(2):
                        up_ref[t, side, 2 * y + py, pl.ds(px, WL, stride=2), :] = phase[
                            row : row + WL, side * 128 : (side + 1) * 128
                        ]
    stores = []
    for t in range(3):
        out_ref[t, 0, :, :, 0:128] = up_ref[t, 0].astype(bf16)
        out_ref[t, 0, :, :, 128:C_UP] = up_ref[t, 1, :, :, 0 : C_UP - 128].astype(bf16)
        stores.append(pltpu.make_async_copy(out_ref.at[t], out_hbm.at[t], sem.at[t]))
        stores[-1].start()
    for store in stores:
        store.wait()


def on_device(
    latent, conv_in_weight, conv_in_bias, first_gain, conv_weight, conv_bias, up_weight, up_bias
):
    w1 = conv_in_weight.reshape(27 * LAT_C, C)
    w2 = pltpu.with_memory_space_constraint(conv_weight.reshape(3, 9 * C, C), pltpu.HBM)
    own, last = pl.pallas_call(
        assemble,
        out_shape=[jax.ShapeDtypeStruct((M0 // 2, 128), bf16), jax.ShapeDtypeStruct((M0 // 8, 128), bf16)],
        in_specs=[VMEM],
        out_specs=[VMEM, VMEM],
        compiler_params=pltpu.CompilerParams(vmem_limit_bytes=8 * 2**20),
        cost_estimate=pl.CostEstimate(flops=10**8, bytes_accessed=10**6, transcendentals=0),
        name="assemble",
    )(gather(latent))
    count = lax.axis_size("tm")
    before = lax.ppermute(own, "tm", [(i, (i + 1) % count) for i in range(count)])
    older = lax.ppermute(last, "tm", [(i, (i + 2) % count) for i in range(count)])
    acc4, tu, w2 = pl.pallas_call(
        front,
        out_shape=[
            jax.ShapeDtypeStruct((M2, C), f32),
            jax.ShapeDtypeStruct((4, 4 * C, 256), bf16),
            pltpu.VMEM((3, 9 * C, C), bf16),
        ],
        in_specs=[VMEM, VMEM, VMEM, HBM, VMEM, VMEM, VMEM],
        out_specs=[VMEM, VMEM, VMEM],
        scratch_shapes=[
            pltpu.VMEM((3 * 256, C), bf16),
            pltpu.SemaphoreType.DMA((3,)),
            pltpu.VMEM((M0 + 8, 128), f32),
            pltpu.VMEM((M0, 256), bf16),
            pltpu.VMEM((M1 + 8, C), f32),
            pltpu.VMEM((M1, 3 * C), bf16),
        ],
        compiler_params=pltpu.CompilerParams(vmem_limit_bytes=24 * 2**20),
        cost_estimate=pl.CostEstimate(flops=10**9, bytes_accessed=10_000_000, transcendentals=10**6),
        name="front",
    )(own, w1, up_weight.transpose(0, 1, 3, 2).reshape(9, C_UP, C), w2, conv_in_bias, first_gain, conv_bias)
    return pl.pallas_call(
        back,
        out_shape=jax.ShapeDtypeStruct((3, 1, 2 * HL, 2 * WL, C_UP), bf16),
        in_specs=[VMEM] * 11,
        out_specs=HBM,
        scratch_shapes=[
            pltpu.VMEM((3 * 256, 2 * C), bf16),
            pltpu.SemaphoreType.DMA((3,)),
            pltpu.VMEM((M0 + 8, 128), f32),
            pltpu.VMEM((2, M0, 256), bf16),
            pltpu.VMEM((4, M1 + 8, C), f32),
            pltpu.VMEM((4, M1, 3 * C), bf16),
            pltpu.VMEM((M2, 3 * C), f32),
            pltpu.VMEM((3, M2, 3 * C), bf16),
            pltpu.VMEM((3, 2, 2 * HL, 2 * WL, 128), f32),
            pltpu.VMEM((3, 1, 2 * HL, 2 * WL, C_UP), bf16),
        ],
        compiler_params=pltpu.CompilerParams(vmem_limit_bytes=32 * 2**20),
        cost_estimate=pl.CostEstimate(flops=8 * 10**9, bytes_accessed=12_000_000, transcendentals=10**6),
        name="back",
    )(own, before, older, acc4, w1, tu, w2, conv_in_bias, first_gain, conv_bias, up_bias)


def solution(mesh):
    return jax.shard_map(
        on_device,
        mesh=mesh,
        in_specs=(P("tm", "tile", None), P(), P(), P(), P(), P(), P(), P()),
        out_specs=P("tm", "tile", None, None, None),
        check_vma=False,
    )
```

```python
import jax
import jax.numpy as jnp
from jax import lax
from jax.experimental import pallas as pl
from jax.experimental.pallas import tpu as pltpu
from jax.sharding import PartitionSpec as P

LAT_C = 16
C = 384
C_UP = 192
HL = 8
WL = 24
GRID = 8
S = 32
M0, M1 = 14 * S, 12 * S
EDGES = 24
CORE, M2, M3 = 10 * WL, 10 * WL + EDGES, HL * WL
bf16, f32 = jnp.bfloat16, jnp.float32
VMEM = pl.BlockSpec(memory_space=pltpu.VMEM)
HBM = pl.BlockSpec(memory_space=pltpu.HBM)


def gather(latent):
    tiles = latent.reshape(3, 3, GRID, GRID, LAT_C).transpose(2, 3, 1, 0, 4)
    tiles = jnp.concatenate([tiles, tiles[:, :, :, 2:]], axis=3).reshape(GRID, GRID, 3 * 64)
    index = lax.axis_index("tile")
    r, g = index // GRID, index % GRID
    side = jnp.where(g < 4, jnp.roll(tiles, -1, axis=1), jnp.roll(tiles, 1, axis=1))
    wide = jnp.concatenate([tiles, side], axis=2)
    other = jnp.where(r < 4, jnp.roll(wide, -1, axis=0), jnp.roll(wide, 1, axis=0))
    pieces = jnp.stack([wide, other], axis=2).reshape(GRID * GRID, 2, 6 * 64)
    own = lax.all_to_all(pieces, "tile", split_axis=0, concat_axis=0, tiled=True)
    return own.reshape(GRID * GRID * 2, 6 * 64)


def place(shape, dim):
    return lax.broadcasted_iota(jnp.int32, shape, dim)


def origin():
    tile = lax.axis_index("tile")
    return lax.div(tile, GRID), lax.rem(tile, GRID)


def inside(rows, margin):
    a, b = origin()
    position = place((rows, 1), 0)
    row = (position >> 5) + a * HL - margin
    column = (position & 31) + b * WL - margin
    return (row >= 0) & (row < GRID * HL) & (column >= 0) & (column < GRID * WL)


def assemble(pieces_ref, own_ref, last_ref):
    a, b = origin()
    parts = []
    for j in range(3):
        group = pieces_ref[:, j * 128 : (j + 1) * 128].astype(f32)
        parts += [group, pltpu.roll(group, 64, 1)]
    stacked = jnp.concatenate(
        [parts[h * 3 + cell].astype(bf16) for cell in range(3) for h in range(2)], axis=0
    )
    row = place((M0, 1), 0)
    big_r, col = row >> 5, row & 31
    group = (col * 43) >> 7
    cell = col - 3 * group
    r = (big_r + 5) & 7
    g = (group + 7) & 7
    outer_r = jnp.where((big_r < 3) | (big_r >= 11), 1, 0)
    outer_g = jnp.where((group == 0) | (group == 9), 1, 0)
    source = cell * 256 + outer_g * 128 + r * 16 + g * 2 + outer_r
    source = jnp.where(inside(M0, 3) & (col < 30), source, -1)
    pick = jnp.where(place((M0, 768), 1) == source, 1.0, 0.0).astype(bf16)
    field = jnp.dot(pick, stacked, preferred_element_type=f32)
    half = M0 // 2
    lane = place((half, 128), 1)
    own_ref[...] = jnp.where(lane < 64, field[:half], pltpu.roll(field[half:], 64, 1)).astype(bf16)
    part = M0 // 8
    lane = place((part, 128), 1) >> 4
    last = jnp.zeros((part, 128), f32)
    for i in range(8):
        shift = (16 * i - 32) % 128
        rows = field[i * part : (i + 1) * part]
        last = jnp.where(lane == i, pltpu.roll(rows, shift, 1) if shift else rows, last)
    last_ref[...] = last.astype(bf16)


def side_by_side(x_ref, shift, target):
    low = place((M0, 128), 1) < 64
    left, middle, right = [
        pltpu.roll(x_ref[pl.ds(dx, M0), :], (64 * (dx % 2) + shift) % 128, 1) for dx in range(3)
    ]
    target[:, 0:128] = jnp.where(low, left, middle).astype(bf16)
    target[:, 128:256] = right.astype(bf16)


def taps(w1_ref, t1_ref, frames):
    t1_ref[...] = jnp.zeros(t1_ref.shape, t1_ref.dtype)
    for tap in range(9):
        for dt in range(3):
            for frame in range(frames):
                row = (tap // 3) * 256 + (tap % 3) * 64 + (frame + dt) * LAT_C
                source = (dt * 9 + tap) * LAT_C
                t1_ref[row : row + LAT_C, frame * C : (frame + 1) * C] = w1_ref[source : source + LAT_C, :]


def rows_of(ref, height):
    return jnp.concatenate([ref[dy * S : dy * S + height, :] for dy in range(3)], axis=1)


def lanes(l, first=0):
    return slice(first + l * 128, first + (l + 1) * 128)


def strip(ref, l, first, height):
    return jnp.concatenate([ref[l, pl.ds(first + y * S, WL), :] for y in range(height)], axis=0)


def edge(ref, l, first, rim_ref):
    for s in range(2):
        rim_ref[pl.ds(s, 10, stride=2), :] = ref[l, pl.ds(first + 25 * s, 10, stride=S), :]
    return rim_ref[...]


def silu_of_norm(start, gain):
    scaling = lax.rsqrt(jnp.mean(start * start, axis=1, keepdims=True) + 1e-06)
    value = start * scaling * gain
    return value / (1.0 + jnp.exp(-value))


def residual(start, b2, act_ref, rim_ref, target, first):
    for l in range(3):
        act_ref[l] = start[:, lanes(l)]
        target[0:CORE, lanes(l, first)] = strip(act_ref, l, S + 2, 10) + b2[:, lanes(l)]
        target[CORE:M2, lanes(l, first)] = edge(act_ref, l, S + 1, rim_ref.at[27 + l]) + b2[:, lanes(l)]


def activate(start, gain, keep, act_ref, rim_ref, la_ref, le_ref):
    value = jnp.where(keep, silu_of_norm(start, gain), 0.0)
    for l in range(3):
        act_ref[l] = value[:, lanes(l)]
        for dx in range(3):
            for y in range(0, 12, 2):
                la_ref[y * WL : (y + 2) * WL, lanes(l, dx * C)] = strip(act_ref, l, y * S + 1 + dx, 2).astype(bf16)
            for dy in range(3):
                rim = edge(act_ref, l, dy * S + dx, rim_ref.at[(dy * 3 + dx) * 3 + l])
                le_ref[:, lanes(l, (dy * 3 + dx) * C)] = rim.astype(bf16)


def taps_of(la_ref, le_ref):
    core = jnp.concatenate([la_ref[dy * WL : dy * WL + CORE, :] for dy in range(3)], axis=1)
    return jnp.concatenate([core, le_ref[...]], axis=0)


def front(
    own_ref, w1_ref, up_ref, w2_hbm, b1_ref, gain_ref, b2_ref, acc_ref, tu_ref, w2_ref,
    t1_ref, sem, x_ref, l1_ref, act_ref, la_ref,
):
    loads = [pltpu.make_async_copy(w2_hbm.at[dt], w2_ref.at[dt], sem.at[dt]) for dt in (2, 0, 1)]
    for load in loads:
        load.start()
    b1, gain, b2 = [ref[...].reshape(1, C) for ref in (b1_ref, gain_ref, b2_ref)]
    taps(w1_ref, t1_ref, 1)
    half = M0 // 2
    packed = own_ref[...].astype(f32)
    x_ref[0:half, :] = packed
    x_ref[half:M0, :] = pltpu.roll(packed, 64, 1)
    x_ref[M0 : M0 + 8, :] = jnp.zeros((8, 128), f32)
    side_by_side(x_ref, 0, l1_ref)
    field = jnp.dot(rows_of(l1_ref, M1), t1_ref[...], preferred_element_type=f32) + b1
    start = field.astype(bf16).astype(f32)
    act_ref[0:M1, :] = start
    kept = act_ref[pl.ds(S + 1, 10 * S), :] + b2
    act_ref[0:M1, :] = jnp.where(inside(M1, 2), silu_of_norm(start, gain), 0.0)
    act_ref[M1 : M1 + 8, :] = jnp.zeros((8, C), f32)
    for dx in range(3):
        la_ref[:, dx * C : (dx + 1) * C] = act_ref[pl.ds(dx, M1), :].astype(bf16)
    groups = (((0,), (1, 2)), ((0, 1), (2,)))
    for py in range(2):
        for px in range(2):
            for ey in range(2):
                for ex in range(2):
                    total = None
                    for dy in groups[py][ey]:
                        for dx in groups[px][ex]:
                            part = up_ref[dy * 3 + dx].astype(f32)
                            total = part if total is None else total + part
                    row = (ey * 2 + ex) * C
                    tu_ref[py * 2 + px, row : row + C, 0:C_UP] = total.T.astype(bf16)
            tu_ref[py * 2 + px, :, C_UP:256] = jnp.zeros((4 * C, 256 - C_UP), bf16)
    loads[0].wait()
    field = kept + jnp.dot(rows_of(la_ref, 10 * S), w2_ref[2], preferred_element_type=f32)
    for l in range(3):
        acc_ref[l] = field[:, lanes(l)]
    for load in loads[1:]:
        load.wait()


def back(
    own_ref, before_ref, older_ref, acc4_ref, w1_ref, tu_ref, w2_ref, b1_ref, gain_ref, b2_ref, bu_ref, out_hbm,
    t1_ref, sem, x_ref, l1_ref, act_ref, rim_ref, la_ref, le_ref, acc_ref, lh_ref, up_ref, out_ref,
):
    b1, gain, b2 = [ref[...].reshape(1, C) for ref in (b1_ref, gain_ref, b2_ref)]
    bu = jnp.concatenate([bu_ref[...].reshape(1, C_UP), jnp.zeros((1, 256 - C_UP), f32)], axis=1)

    half, part = M0 // 2, M0 // 8
    x = lax.axis_index("tm")
    now, before, older = [
        jnp.where(x >= d, ref[...].astype(f32), 0.0) for d, ref in enumerate((own_ref, before_ref, older_ref))
    ]
    lane = place((half, 128), 1)
    for i in range(2):
        past = pltpu.roll(before, 64, 1) if i else before
        old = jnp.concatenate([pltpu.roll(older, 112 - 16 * (4 * i + k), 1) if 4 * i + k < 7 else older for k in range(4)], axis=0)
        x_ref[i * half : (i + 1) * half, :] = jnp.where(
            lane < 48, past, jnp.where(lane < 96, pltpu.roll(now, 112 if i else 48, 1), old)
        )
    x_ref[M0 : M0 + 8, :] = jnp.zeros((8, 128), f32)
    taps(w1_ref, t1_ref, 2)

    rim_ref[...] = jnp.zeros(rim_ref.shape, f32)
    keep = inside(M1, 2)
    for pair in range(2):
        side_by_side(x_ref, (16 - 32 * pair) % 128, l1_ref.at[pair])
        fields = jnp.dot(rows_of(l1_ref.at[pair], M1), t1_ref[...], preferred_element_type=f32)
        for k in range(2):
            frame = 2 * pair + k
            start = (fields[:, k * C : (k + 1) * C] + b1).astype(bf16).astype(f32)
            if pair:
                residual(start, b2, act_ref.at[frame], rim_ref.at[frame], acc_ref, k * C)
            activate(
                start, gain, keep if pair else keep & (x > 0), act_ref.at[frame], rim_ref.at[frame],
                la_ref.at[frame], le_ref.at[frame],
            )
    for l in range(3):
        acc_ref[0:CORE, lanes(l, 2 * C)] = strip(acc4_ref, l, 1, 10)
        acc_ref[CORE:M2, lanes(l, 2 * C)] = edge(acc4_ref, l, 0, rim_ref.at[0, 27 + l])

    for frame in range(4):
        low, high = max(0, frame - 2), min(2, frame)
        weight = jnp.concatenate([w2_ref[frame - t] for t in range(low, high + 1)], axis=1)
        acc_ref[:, low * C : (high + 1) * C] += jnp.dot(
            taps_of(la_ref.at[frame], le_ref.at[frame]), weight, preferred_element_type=f32
        )

    a, b = origin()
    position = place((M2, 1), 0)
    core = position < CORE
    row = jnp.where(core, (position * 2731) >> 16, (position - CORE) >> 1) + a * HL - 1
    column = jnp.where(core, 0, b * WL - 1 + 25 * (position & 1))
    keep = (row >= 0) & (row < GRID * HL) & (column >= 0) & (column < GRID * WL)
    for t in range(3):
        for l in range(3):
            act, rim = act_ref.at[t], rim_ref.at[t]
            field = jnp.where(keep, acc_ref[:, lanes(l, t * C)], 0.0)
            for y in range(10):
                act[l, pl.ds(y * S + 1, WL), :] = field[y * WL : (y + 1) * WL]
            rim[l] = field[CORE:M2]
            for s in range(2):
                act[l, pl.ds(25 * s, 10, stride=S), :] = rim[l, pl.ds(s, 10, stride=2), :]
            for dx in range(3):
                for y in range(0, 10, 2):
                    lh_ref[t, y * WL : (y + 2) * WL, lanes(l, dx * C)] = strip(act, l, y * S + dx, 2).astype(bf16)
    for py in range(2):
        for px in range(2):
            lhs = jnp.concatenate(
                [
                    jnp.concatenate(
                        [
                            lh_ref[t, (py + ey) * WL : (py + ey) * WL + M3, (px + ex) * C : (px + ex + 1) * C]
                            for t in range(3)
                        ],
                        axis=0,
                    )
                    for ey in range(2)
                    for ex in range(2)
                ],
                axis=1,
            )
            phase = jnp.dot(lhs, tu_ref[py * 2 + px], preferred_element_type=f32) + bu
            for t in range(3):
                for y in range(HL):
                    row = t * M3 + y * WL
                    for side in range(2):
                        up_ref[t, side, 2 * y + py, pl.ds(px, WL, stride=2), :] = phase[
                            row : row + WL, side * 128 : (side + 1) * 128
                        ]
    stores = []
    for t in range(3):
        out_ref[t, 0, :, :, 0:128] = up_ref[t, 0].astype(bf16)
        out_ref[t, 0, :, :, 128:C_UP] = up_ref[t, 1, :, :, 0 : C_UP - 128].astype(bf16)
        stores.append(pltpu.make_async_copy(out_ref.at[t], out_hbm.at[t], sem.at[t]))
        stores[-1].start()
    for store in stores:
        store.wait()


def on_device(
    latent, conv_in_weight, conv_in_bias, first_gain, conv_weight, conv_bias, up_weight, up_bias
):
    w1 = conv_in_weight.reshape(27 * LAT_C, C)
    w2 = pltpu.with_memory_space_constraint(conv_weight.reshape(3, 9 * C, C), pltpu.HBM)
    own, last = pl.pallas_call(
        assemble,
        out_shape=[jax.ShapeDtypeStruct((M0 // 2, 128), bf16), jax.ShapeDtypeStruct((M0 // 8, 128), bf16)],
        in_specs=[VMEM],
        out_specs=[VMEM, VMEM],
        compiler_params=pltpu.CompilerParams(vmem_limit_bytes=8 * 2**20),
        cost_estimate=pl.CostEstimate(flops=10**8, bytes_accessed=10**6, transcendentals=0),
        name="assemble",
    )(gather(latent))
    count = lax.axis_size("tm")
    before = lax.ppermute(own, "tm", [(i, (i + 1) % count) for i in range(count)])
    older = lax.ppermute(last, "tm", [(i, (i + 2) % count) for i in range(count)])
    acc4, tu, w2 = pl.pallas_call(
        front,
        out_shape=[
            jax.ShapeDtypeStruct((3, 10 * S, 128), f32),
            jax.ShapeDtypeStruct((4, 4 * C, 256), bf16),
            pltpu.VMEM((3, 9 * C, C), bf16),
        ],
        in_specs=[VMEM, VMEM, VMEM, HBM, VMEM, VMEM, VMEM],
        out_specs=[VMEM, VMEM, VMEM],
        scratch_shapes=[
            pltpu.VMEM((3 * 256, C), bf16),
            pltpu.SemaphoreType.DMA((3,)),
            pltpu.VMEM((M0 + 8, 128), f32),
            pltpu.VMEM((M0, 256), bf16),
            pltpu.VMEM((M1 + 8, C), f32),
            pltpu.VMEM((M1, 3 * C), bf16),
        ],
        compiler_params=pltpu.CompilerParams(vmem_limit_bytes=24 * 2**20),
        cost_estimate=pl.CostEstimate(flops=10**9, bytes_accessed=10_000_000, transcendentals=10**6),
        name="front",
    )(own, w1, up_weight.transpose(0, 1, 3, 2).reshape(9, C_UP, C), w2, conv_in_bias, first_gain, conv_bias)
    return pl.pallas_call(
        back,
        out_shape=jax.ShapeDtypeStruct((3, 1, 2 * HL, 2 * WL, C_UP), bf16),
        in_specs=[VMEM] * 11,
        out_specs=HBM,
        scratch_shapes=[
            pltpu.VMEM((3 * 256, 2 * C), bf16),
            pltpu.SemaphoreType.DMA((3,)),
            pltpu.VMEM((M0 + 8, 128), f32),
            pltpu.VMEM((2, M0, 256), bf16),
            pltpu.VMEM((4, 3, M1, 128), f32),
            pltpu.VMEM((4, 30, EDGES, 128), f32),
            pltpu.VMEM((4, 12 * WL, 3 * C), bf16),
            pltpu.VMEM((4, EDGES, 9 * C), bf16),
            pltpu.VMEM((M2, 3 * C), f32),
            pltpu.VMEM((3, CORE, 3 * C), bf16),
            pltpu.VMEM((3, 2, 2 * HL, 2 * WL, 128), f32),
            pltpu.VMEM((3, 1, 2 * HL, 2 * WL, C_UP), bf16),
        ],
        compiler_params=pltpu.CompilerParams(vmem_limit_bytes=32 * 2**20),
        cost_estimate=pl.CostEstimate(flops=8 * 10**9, bytes_accessed=12_000_000, transcendentals=10**6),
        name="back",
    )(own, before, older, acc4, w1, tu, w2, conv_in_bias, first_gain, conv_bias, up_bias)


def solution(mesh):
    return jax.shard_map(
        on_device,
        mesh=mesh,
        in_specs=(P("tm", "tile", None), P(), P(), P(), P(), P(), P(), P()),
        out_specs=P("tm", "tile", None, None, None),
        check_vma=False,
    )
```

```python
import jax
import jax.numpy as jnp
from jax import lax
from jax.experimental import pallas as pl
from jax.experimental.pallas import tpu as pltpu
from jax.sharding import PartitionSpec as P

LAT_C = 16
C = 384
C_UP = 192
HL = 8
WL = 24
GRID = 8
S = 32
M0, M1 = 14 * S, 12 * S
EDGES = 24
CORE, M2, M3 = 10 * WL, 10 * WL + EDGES, HL * WL
bf16, f32 = jnp.bfloat16, jnp.float32
VMEM = pl.BlockSpec(memory_space=pltpu.VMEM)
HBM = pl.BlockSpec(memory_space=pltpu.HBM)


def gather(latent):
    pieces = pl.pallas_call(
        deal,
        out_shape=jax.ShapeDtypeStruct((2 * GRID * GRID, 6 * 64), bf16),
        in_specs=[HBM],
        out_specs=VMEM,
        scratch_shapes=[
            pltpu.VMEM(latent.shape, bf16),
            pltpu.VMEM((3, 2 * GRID * GRID, 128), f32),
            pltpu.SemaphoreType.DMA,
        ],
        compiler_params=pltpu.CompilerParams(vmem_limit_bytes=8 * 2**20),
        cost_estimate=pl.CostEstimate(flops=10**9, bytes_accessed=10**7, transcendentals=0),
        name="deal",
    )(pltpu.with_memory_space_constraint(latent, pltpu.HBM))
    pieces = pieces.reshape(GRID * GRID, 2, 6 * 64)
    own = lax.all_to_all(pieces, "tile", split_axis=0, concat_axis=0, tiled=True)
    return own.reshape(GRID * GRID * 2, 6 * 64)


def place(shape, dim):
    return lax.broadcasted_iota(jnp.int32, shape, dim)


def origin():
    tile = lax.axis_index("tile")
    return lax.div(tile, GRID), lax.rem(tile, GRID)


def deal(latent_hbm, out_ref, latent_ref, rows_ref, sem):
    load = pltpu.make_async_copy(latent_hbm, latent_ref, sem)
    load.start()
    r, g = origin()
    source, target = place((3 * 128, 128), 0), place((3 * 128, 128), 1)
    frame = jnp.minimum(target >> 4, 2)
    fold = ((source >> 7) == frame) & ((source & 15) == (target & 15)) & (target < 64)
    fold = jnp.where(fold, 1.0, 0.0).astype(bf16)
    load.wait()
    own = (place((GRID, 128), 1) >> 4) == place((GRID, 128), 0)
    spread = []
    for cell in range(3):
        blocks = []
        for frame in range(3):
            row = latent_ref[frame, pl.ds(cell, 1), :].astype(f32)
            blocks.append(
                jnp.concatenate(
                    [
                        jnp.where(own, jnp.broadcast_to(row[:, a * 128 : (a + 1) * 128], (GRID, 128)), 0.0)
                        for a in range(GRID)
                    ],
                    axis=0,
                )
            )
        spread.append(jnp.concatenate(blocks, axis=1))
    spread = jnp.concatenate(spread, axis=0).astype(bf16)
    cells = jnp.dot(spread, fold, preferred_element_type=f32)
    count = GRID * GRID
    cells = [cells[cell * count : (cell + 1) * count] for cell in range(3)]
    sides = [
        jnp.concatenate(
            [
                jnp.where(g < 4, pltpu.roll(row, 7, 0), pltpu.roll(row, 1, 0))
                for row in (field[a * GRID : (a + 1) * GRID] for a in range(GRID))
            ],
            axis=0,
        )
        for field in cells
    ]
    groups = cells + sides
    low = place((count, 128), 1) < 64
    for j in range(3):
        wide = jnp.where(low, groups[2 * j], pltpu.roll(groups[2 * j + 1], 64, 1))
        above = jnp.concatenate([wide[GRID:], wide[:GRID]], axis=0)
        below = jnp.concatenate([wide[-GRID:], wide[:-GRID]], axis=0)
        rows_ref[j, pl.ds(0, count, stride=2), :] = wide
        rows_ref[j, pl.ds(1, count, stride=2), :] = jnp.where(r < 4, above, below)
        out_ref[:, j * 128 : (j + 1) * 128] = rows_ref[j].astype(bf16)


def inside(rows, margin):
    a, b = origin()
    position = place((rows, 1), 0)
    row = (position >> 5) + a * HL - margin
    column = (position & 31) + b * WL - margin
    return (row >= 0) & (row < GRID * HL) & (column >= 0) & (column < GRID * WL)


def assemble(pieces_ref, own_ref, last_ref):
    a, b = origin()
    parts = []
    for j in range(3):
        group = pieces_ref[:, j * 128 : (j + 1) * 128].astype(f32)
        parts += [group, pltpu.roll(group, 64, 1)]
    stacked = jnp.concatenate(
        [parts[h * 3 + cell].astype(bf16) for cell in range(3) for h in range(2)], axis=0
    )
    row = place((M0, 1), 0)
    big_r, col = row >> 5, row & 31
    group = (col * 43) >> 7
    cell = col - 3 * group
    r = (big_r + 5) & 7
    g = (group + 7) & 7
    outer_r = jnp.where((big_r < 3) | (big_r >= 11), 1, 0)
    outer_g = jnp.where((group == 0) | (group == 9), 1, 0)
    source = cell * 256 + outer_g * 128 + r * 16 + g * 2 + outer_r
    source = jnp.where(inside(M0, 3) & (col < 30), source, -1)
    pick = jnp.where(place((M0, 768), 1) == source, 1.0, 0.0).astype(bf16)
    field = jnp.dot(pick, stacked, preferred_element_type=f32)
    half = M0 // 2
    lane = place((half, 128), 1)
    own_ref[...] = jnp.where(lane < 64, field[:half], pltpu.roll(field[half:], 64, 1)).astype(bf16)
    part = M0 // 8
    lane = place((part, 128), 1) >> 4
    last = jnp.zeros((part, 128), f32)
    for i in range(8):
        shift = (16 * i - 32) % 128
        rows = field[i * part : (i + 1) * part]
        last = jnp.where(lane == i, pltpu.roll(rows, shift, 1) if shift else rows, last)
    last_ref[...] = last.astype(bf16)


def side_by_side(x_ref, shift, target):
    low = place((M0, 128), 1) < 64
    left, middle, right = [
        pltpu.roll(x_ref[pl.ds(dx, M0), :], (64 * (dx % 2) + shift) % 128, 1) for dx in range(3)
    ]
    target[:, 0:128] = jnp.where(low, left, middle).astype(bf16)
    target[:, 128:256] = right.astype(bf16)


def taps(w1_ref, t1_ref, frames):
    t1_ref[...] = jnp.zeros(t1_ref.shape, t1_ref.dtype)
    for tap in range(9):
        for dt in range(3):
            for frame in range(frames):
                row = (tap // 3) * 256 + (tap % 3) * 64 + (frame + dt) * LAT_C
                source = (dt * 9 + tap) * LAT_C
                t1_ref[row : row + LAT_C, frame * C : (frame + 1) * C] = w1_ref[source : source + LAT_C, :]


def rows_of(ref, height):
    return jnp.concatenate([ref[dy * S : dy * S + height, :] for dy in range(3)], axis=1)


def lanes(l, first=0):
    return slice(first + l * 128, first + (l + 1) * 128)


def strip(ref, l, first, height):
    return jnp.concatenate([ref[l, pl.ds(first + y * S, WL), :] for y in range(height)], axis=0)


def edge(ref, l, first, rim_ref):
    for s in range(2):
        rim_ref[pl.ds(s, 10, stride=2), :] = ref[l, pl.ds(first + 25 * s, 10, stride=S), :]
    return rim_ref[...]


def silu_of_norm(start, gain):
    scaling = lax.rsqrt(jnp.mean(start * start, axis=1, keepdims=True) + 1e-06)
    value = start * scaling * gain
    return value / (1.0 + jnp.exp(-value))


def residual(start, b2, act_ref, rim_ref, target, first):
    for l in range(3):
        act_ref[l] = start[:, lanes(l)]
        target[0:CORE, lanes(l, first)] = strip(act_ref, l, S + 2, 10) + b2[:, lanes(l)]
        target[CORE:M2, lanes(l, first)] = edge(act_ref, l, S + 1, rim_ref.at[27 + l]) + b2[:, lanes(l)]


def activate(start, gain, keep, act_ref, rim_ref, la_ref, le_ref):
    value = jnp.where(keep, silu_of_norm(start, gain), 0.0)
    for l in range(3):
        act_ref[l] = value[:, lanes(l)]
        for dx in range(3):
            for y in range(0, 12, 2):
                la_ref[y * WL : (y + 2) * WL, lanes(l, dx * C)] = strip(act_ref, l, y * S + 1 + dx, 2).astype(bf16)
            for dy in range(3):
                rim = edge(act_ref, l, dy * S + dx, rim_ref.at[(dy * 3 + dx) * 3 + l])
                le_ref[:, lanes(l, (dy * 3 + dx) * C)] = rim.astype(bf16)


def taps_of(la_ref, le_ref):
    core = jnp.concatenate([la_ref[dy * WL : dy * WL + CORE, :] for dy in range(3)], axis=1)
    return jnp.concatenate([core, le_ref[...]], axis=0)


def front(
    own_ref, w1_ref, up_ref, w2_hbm, b1_ref, gain_ref, b2_ref, acc_ref, tu_ref, w2_ref,
    t1_ref, sem, x_ref, l1_ref, act_ref, la_ref,
):
    loads = [pltpu.make_async_copy(w2_hbm.at[dt], w2_ref.at[dt], sem.at[dt]) for dt in (2, 0, 1)]
    for load in loads:
        load.start()
    b1, gain, b2 = [ref[...].reshape(1, C) for ref in (b1_ref, gain_ref, b2_ref)]
    taps(w1_ref, t1_ref, 1)
    half = M0 // 2
    packed = own_ref[...].astype(f32)
    x_ref[0:half, :] = packed
    x_ref[half:M0, :] = pltpu.roll(packed, 64, 1)
    x_ref[M0 : M0 + 8, :] = jnp.zeros((8, 128), f32)
    side_by_side(x_ref, 0, l1_ref)
    field = jnp.dot(rows_of(l1_ref, M1), t1_ref[...], preferred_element_type=f32) + b1
    start = field.astype(bf16).astype(f32)
    act_ref[0:M1, :] = start
    kept = act_ref[pl.ds(S + 1, 10 * S), :] + b2
    act_ref[0:M1, :] = jnp.where(inside(M1, 2), silu_of_norm(start, gain), 0.0)
    act_ref[M1 : M1 + 8, :] = jnp.zeros((8, C), f32)
    for dx in range(3):
        la_ref[:, dx * C : (dx + 1) * C] = act_ref[pl.ds(dx, M1), :].astype(bf16)
    groups = (((0,), (1, 2)), ((0, 1), (2,)))
    for py in range(2):
        for px in range(2):
            for ey in range(2):
                for ex in range(2):
                    total = None
                    for dy in groups[py][ey]:
                        for dx in groups[px][ex]:
                            part = up_ref[dy * 3 + dx].astype(f32)
                            total = part if total is None else total + part
                    row = (ey * 2 + ex) * C
                    tu_ref[py * 2 + px, row : row + C, 0:C_UP] = total.T.astype(bf16)
            tu_ref[py * 2 + px, :, C_UP:256] = jnp.zeros((4 * C, 256 - C_UP), bf16)
    loads[0].wait()
    field = kept + jnp.dot(rows_of(la_ref, 10 * S), w2_ref[2], preferred_element_type=f32)
    for l in range(3):
        acc_ref[l] = field[:, lanes(l)]
    for load in loads[1:]:
        load.wait()


def back(
    own_ref, before_ref, older_ref, acc4_ref, w1_ref, tu_ref, w2_ref, b1_ref, gain_ref, b2_ref, bu_ref, out_hbm,
    t1_ref, sem, x_ref, l1_ref, act_ref, rim_ref, la_ref, le_ref, acc_ref, lh_ref, up_ref, out_ref,
):
    b1, gain, b2 = [ref[...].reshape(1, C) for ref in (b1_ref, gain_ref, b2_ref)]
    bu = jnp.concatenate([bu_ref[...].reshape(1, C_UP), jnp.zeros((1, 256 - C_UP), f32)], axis=1)

    half, part = M0 // 2, M0 // 8
    x = lax.axis_index("tm")
    now, before, older = [
        jnp.where(x >= d, ref[...].astype(f32), 0.0) for d, ref in enumerate((own_ref, before_ref, older_ref))
    ]
    lane = place((half, 128), 1)
    for i in range(2):
        past = pltpu.roll(before, 64, 1) if i else before
        old = jnp.concatenate([pltpu.roll(older, 112 - 16 * (4 * i + k), 1) if 4 * i + k < 7 else older for k in range(4)], axis=0)
        x_ref[i * half : (i + 1) * half, :] = jnp.where(
            lane < 48, past, jnp.where(lane < 96, pltpu.roll(now, 112 if i else 48, 1), old)
        )
    x_ref[M0 : M0 + 8, :] = jnp.zeros((8, 128), f32)
    taps(w1_ref, t1_ref, 2)

    rim_ref[...] = jnp.zeros(rim_ref.shape, f32)
    keep = inside(M1, 2)
    for pair in range(2):
        side_by_side(x_ref, (16 - 32 * pair) % 128, l1_ref.at[pair])
        fields = jnp.dot(rows_of(l1_ref.at[pair], M1), t1_ref[...], preferred_element_type=f32)
        for k in range(2):
            frame = 2 * pair + k
            start = (fields[:, k * C : (k + 1) * C] + b1).astype(bf16).astype(f32)
            if pair:
                residual(start, b2, act_ref.at[frame], rim_ref.at[frame], acc_ref, k * C)
            activate(
                start, gain, keep if pair else keep & (x > 0), act_ref.at[frame], rim_ref.at[frame],
                la_ref.at[frame], le_ref.at[frame],
            )
    for l in range(3):
        acc_ref[0:CORE, lanes(l, 2 * C)] = strip(acc4_ref, l, 1, 10)
        acc_ref[CORE:M2, lanes(l, 2 * C)] = edge(acc4_ref, l, 0, rim_ref.at[0, 27 + l])

    for frame in range(4):
        low, high = max(0, frame - 2), min(2, frame)
        weight = jnp.concatenate([w2_ref[frame - t] for t in range(low, high + 1)], axis=1)
        acc_ref[:, low * C : (high + 1) * C] += jnp.dot(
            taps_of(la_ref.at[frame], le_ref.at[frame]), weight, preferred_element_type=f32
        )

    a, b = origin()
    position = place((M2, 1), 0)
    core = position < CORE
    row = jnp.where(core, (position * 2731) >> 16, (position - CORE) >> 1) + a * HL - 1
    column = jnp.where(core, 0, b * WL - 1 + 25 * (position & 1))
    keep = (row >= 0) & (row < GRID * HL) & (column >= 0) & (column < GRID * WL)
    for t in range(3):
        for l in range(3):
            act, rim = act_ref.at[t], rim_ref.at[t]
            field = jnp.where(keep, acc_ref[:, lanes(l, t * C)], 0.0)
            for y in range(10):
                act[l, pl.ds(y * S + 1, WL), :] = field[y * WL : (y + 1) * WL]
            rim[l] = field[CORE:M2]
            for s in range(2):
                act[l, pl.ds(25 * s, 10, stride=S), :] = rim[l, pl.ds(s, 10, stride=2), :]
            for dx in range(3):
                for y in range(0, 10, 2):
                    lh_ref[t, y * WL : (y + 2) * WL, lanes(l, dx * C)] = strip(act, l, y * S + dx, 2).astype(bf16)
    for py in range(2):
        for px in range(2):
            lhs = jnp.concatenate(
                [
                    jnp.concatenate(
                        [
                            lh_ref[t, (py + ey) * WL : (py + ey) * WL + M3, (px + ex) * C : (px + ex + 1) * C]
                            for t in range(3)
                        ],
                        axis=0,
                    )
                    for ey in range(2)
                    for ex in range(2)
                ],
                axis=1,
            )
            phase = jnp.dot(lhs, tu_ref[py * 2 + px], preferred_element_type=f32) + bu
            for t in range(3):
                for y in range(HL):
                    row = t * M3 + y * WL
                    for side in range(2):
                        up_ref[t, side, 2 * y + py, pl.ds(px, WL, stride=2), :] = phase[
                            row : row + WL, side * 128 : (side + 1) * 128
                        ]
    stores = []
    for t in range(3):
        out_ref[t, 0, :, :, 0:128] = up_ref[t, 0].astype(bf16)
        out_ref[t, 0, :, :, 128:C_UP] = up_ref[t, 1, :, :, 0 : C_UP - 128].astype(bf16)
        stores.append(pltpu.make_async_copy(out_ref.at[t], out_hbm.at[t], sem.at[t]))
        stores[-1].start()
    for store in stores:
        store.wait()


def on_device(
    latent, conv_in_weight, conv_in_bias, first_gain, conv_weight, conv_bias, up_weight, up_bias
):
    w1 = conv_in_weight.reshape(27 * LAT_C, C)
    w2 = pltpu.with_memory_space_constraint(conv_weight.reshape(3, 9 * C, C), pltpu.HBM)
    own, last = pl.pallas_call(
        assemble,
        out_shape=[jax.ShapeDtypeStruct((M0 // 2, 128), bf16), jax.ShapeDtypeStruct((M0 // 8, 128), bf16)],
        in_specs=[VMEM],
        out_specs=[VMEM, VMEM],
        compiler_params=pltpu.CompilerParams(vmem_limit_bytes=8 * 2**20),
        cost_estimate=pl.CostEstimate(flops=10**8, bytes_accessed=10**6, transcendentals=0),
        name="assemble",
    )(gather(latent))
    count = lax.axis_size("tm")
    before = lax.ppermute(own, "tm", [(i, (i + 1) % count) for i in range(count)])
    older = lax.ppermute(last, "tm", [(i, (i + 2) % count) for i in range(count)])
    acc4, tu, w2 = pl.pallas_call(
        front,
        out_shape=[
            jax.ShapeDtypeStruct((3, 10 * S, 128), f32),
            jax.ShapeDtypeStruct((4, 4 * C, 256), bf16),
            pltpu.VMEM((3, 9 * C, C), bf16),
        ],
        in_specs=[VMEM, VMEM, VMEM, HBM, VMEM, VMEM, VMEM],
        out_specs=[VMEM, VMEM, VMEM],
        scratch_shapes=[
            pltpu.VMEM((3 * 256, C), bf16),
            pltpu.SemaphoreType.DMA((3,)),
            pltpu.VMEM((M0 + 8, 128), f32),
            pltpu.VMEM((M0, 256), bf16),
            pltpu.VMEM((M1 + 8, C), f32),
            pltpu.VMEM((M1, 3 * C), bf16),
        ],
        compiler_params=pltpu.CompilerParams(vmem_limit_bytes=24 * 2**20),
        cost_estimate=pl.CostEstimate(flops=10**9, bytes_accessed=10_000_000, transcendentals=10**6),
        name="front",
    )(own, w1, up_weight.transpose(0, 1, 3, 2).reshape(9, C_UP, C), w2, conv_in_bias, first_gain, conv_bias)
    return pl.pallas_call(
        back,
        out_shape=jax.ShapeDtypeStruct((3, 1, 2 * HL, 2 * WL, C_UP), bf16),
        in_specs=[VMEM] * 11,
        out_specs=HBM,
        scratch_shapes=[
            pltpu.VMEM((3 * 256, 2 * C), bf16),
            pltpu.SemaphoreType.DMA((3,)),
            pltpu.VMEM((M0 + 8, 128), f32),
            pltpu.VMEM((2, M0, 256), bf16),
            pltpu.VMEM((4, 3, M1, 128), f32),
            pltpu.VMEM((4, 30, EDGES, 128), f32),
            pltpu.VMEM((4, 12 * WL, 3 * C), bf16),
            pltpu.VMEM((4, EDGES, 9 * C), bf16),
            pltpu.VMEM((M2, 3 * C), f32),
            pltpu.VMEM((3, CORE, 3 * C), bf16),
            pltpu.VMEM((3, 2, 2 * HL, 2 * WL, 128), f32),
            pltpu.VMEM((3, 1, 2 * HL, 2 * WL, C_UP), bf16),
        ],
        compiler_params=pltpu.CompilerParams(vmem_limit_bytes=32 * 2**20),
        cost_estimate=pl.CostEstimate(flops=8 * 10**9, bytes_accessed=12_000_000, transcendentals=10**6),
        name="back",
    )(own, before, older, acc4, w1, tu, w2, conv_in_bias, first_gain, conv_bias, up_bias)


def solution(mesh):
    return jax.shard_map(
        on_device,
        mesh=mesh,
        in_specs=(P("tm", "tile", None), P(), P(), P(), P(), P(), P(), P()),
        out_specs=P("tm", "tile", None, None, None),
        check_vma=False,
    )
```

```python
import jax
import jax.numpy as jnp
from jax import lax
from jax.experimental import pallas as pl
from jax.experimental.pallas import tpu as pltpu
from jax.sharding import PartitionSpec as P

LAT_C = 16
C = 384
C_UP = 192
HL = 8
WL = 24
GRID = 8
S = 32
M0, M1 = 14 * S, 12 * S
EDGES = 24
RIM, TALL = 32, 18 * S
CORE, M2, M3 = 10 * WL, 10 * WL + EDGES, HL * WL
bf16, f32 = jnp.bfloat16, jnp.float32
VMEM = pl.BlockSpec(memory_space=pltpu.VMEM)
HBM = pl.BlockSpec(memory_space=pltpu.HBM)


def gather(latent):
    pieces = pl.pallas_call(
        deal,
        out_shape=jax.ShapeDtypeStruct((2 * GRID * GRID, 6 * 64), bf16),
        in_specs=[HBM],
        out_specs=VMEM,
        scratch_shapes=[
            pltpu.VMEM(latent.shape, bf16),
            pltpu.VMEM((3, 2 * GRID * GRID, 128), f32),
            pltpu.SemaphoreType.DMA,
        ],
        compiler_params=pltpu.CompilerParams(vmem_limit_bytes=8 * 2**20),
        cost_estimate=pl.CostEstimate(flops=10**9, bytes_accessed=10**7, transcendentals=0),
        name="deal",
    )(pltpu.with_memory_space_constraint(latent, pltpu.HBM))
    pieces = pieces.reshape(GRID * GRID, 2, 6 * 64)
    own = lax.all_to_all(pieces, "tile", split_axis=0, concat_axis=0, tiled=True)
    return own.reshape(GRID * GRID * 2, 6 * 64)


def place(shape, dim):
    return lax.broadcasted_iota(jnp.int32, shape, dim)


def origin():
    tile = lax.axis_index("tile")
    return lax.div(tile, GRID), lax.rem(tile, GRID)


def deal(latent_hbm, out_ref, latent_ref, rows_ref, sem):
    load = pltpu.make_async_copy(latent_hbm, latent_ref, sem)
    load.start()
    r, g = origin()
    source, target = place((3 * 128, 128), 0), place((3 * 128, 128), 1)
    frame = jnp.minimum(target >> 4, 2)
    fold = ((source >> 7) == frame) & ((source & 15) == (target & 15)) & (target < 64)
    fold = jnp.where(fold, 1.0, 0.0).astype(bf16)
    load.wait()
    own = (place((GRID, 128), 1) >> 4) == place((GRID, 128), 0)
    spread = []
    for cell in range(3):
        blocks = []
        for frame in range(3):
            row = latent_ref[frame, pl.ds(cell, 1), :].astype(f32)
            blocks.append(
                jnp.concatenate(
                    [
                        jnp.where(own, jnp.broadcast_to(row[:, a * 128 : (a + 1) * 128], (GRID, 128)), 0.0)
                        for a in range(GRID)
                    ],
                    axis=0,
                )
            )
        spread.append(jnp.concatenate(blocks, axis=1))
    spread = jnp.concatenate(spread, axis=0).astype(bf16)
    cells = jnp.dot(spread, fold, preferred_element_type=f32)
    count = GRID * GRID
    cells = [cells[cell * count : (cell + 1) * count] for cell in range(3)]
    sides = [
        jnp.concatenate(
            [
                jnp.where(g < 4, pltpu.roll(row, 7, 0), pltpu.roll(row, 1, 0))
                for row in (field[a * GRID : (a + 1) * GRID] for a in range(GRID))
            ],
            axis=0,
        )
        for field in cells
    ]
    groups = cells + sides
    low = place((count, 128), 1) < 64
    for j in range(3):
        wide = jnp.where(low, groups[2 * j], pltpu.roll(groups[2 * j + 1], 64, 1))
        above = jnp.concatenate([wide[GRID:], wide[:GRID]], axis=0)
        below = jnp.concatenate([wide[-GRID:], wide[:-GRID]], axis=0)
        rows_ref[j, pl.ds(0, count, stride=2), :] = wide
        rows_ref[j, pl.ds(1, count, stride=2), :] = jnp.where(r < 4, above, below)
        out_ref[:, j * 128 : (j + 1) * 128] = rows_ref[j].astype(bf16)


def inside(rows, margin):
    a, b = origin()
    position = place((rows, 1), 0)
    row = (position >> 5) + a * HL - margin
    column = (position & 31) + b * WL - margin
    return (row >= 0) & (row < GRID * HL) & (column >= 0) & (column < GRID * WL)


def assemble(pieces_ref, own_ref, last_ref):
    a, b = origin()
    parts = []
    for j in range(3):
        group = pieces_ref[:, j * 128 : (j + 1) * 128].astype(f32)
        parts += [group, pltpu.roll(group, 64, 1)]
    stacked = jnp.concatenate(
        [parts[h * 3 + cell].astype(bf16) for cell in range(3) for h in range(2)], axis=0
    )
    row = place((M0, 1), 0)
    big_r, col = row >> 5, row & 31
    group = (col * 43) >> 7
    cell = col - 3 * group
    r = (big_r + 5) & 7
    g = (group + 7) & 7
    outer_r = jnp.where((big_r < 3) | (big_r >= 11), 1, 0)
    outer_g = jnp.where((group == 0) | (group == 9), 1, 0)
    source = cell * 256 + outer_g * 128 + r * 16 + g * 2 + outer_r
    source = jnp.where(inside(M0, 3) & (col < 30), source, -1)
    pick = jnp.where(place((M0, 768), 1) == source, 1.0, 0.0).astype(bf16)
    field = jnp.dot(pick, stacked, preferred_element_type=f32)
    half = M0 // 2
    lane = place((half, 128), 1)
    own_ref[...] = jnp.where(lane < 64, field[:half], pltpu.roll(field[half:], 64, 1)).astype(bf16)
    part = M0 // 8
    lane = place((part, 128), 1) >> 4
    last = jnp.zeros((part, 128), f32)
    for i in range(8):
        shift = (16 * i - 32) % 128
        rows = field[i * part : (i + 1) * part]
        last = jnp.where(lane == i, pltpu.roll(rows, shift, 1) if shift else rows, last)
    last_ref[...] = last.astype(bf16)


def side_by_side(x_ref, shift, target):
    low = place((M0, 128), 1) < 64
    left, middle, right = [
        pltpu.roll(x_ref[pl.ds(dx, M0), :], (64 * (dx % 2) + shift) % 128, 1) for dx in range(3)
    ]
    target[:, 0:128] = jnp.where(low, left, middle).astype(bf16)
    target[:, 128:256] = right.astype(bf16)


def taps(w1_ref, t1_ref, frames):
    t1_ref[...] = jnp.zeros(t1_ref.shape, t1_ref.dtype)
    for tap in range(9):
        for dt in range(3):
            for frame in range(frames):
                row = (tap // 3) * 256 + (tap % 3) * 64 + (frame + dt) * LAT_C
                source = (dt * 9 + tap) * LAT_C
                t1_ref[row : row + LAT_C, frame * C : (frame + 1) * C] = w1_ref[source : source + LAT_C, :]


def rows_of(ref, height):
    return jnp.concatenate([ref[dy * S : dy * S + height, :] for dy in range(3)], axis=1)


def lanes(l, first=0):
    return slice(first + l * 128, first + (l + 1) * 128)


def strip(ref, l, first, height):
    return jnp.concatenate([ref[l, pl.ds(first + y * S, WL), :] for y in range(height)], axis=0)


def edge(ref, l, first, rim_ref):
    for s in range(2):
        rim_ref[pl.ds(s, 10, stride=2), :] = ref[l, pl.ds(first + 25 * s, 10, stride=S), :]
    return rim_ref[0:EDGES, :]


def silu_of_norm(start, gain):
    scaling = lax.rsqrt(jnp.mean(start * start, axis=1, keepdims=True) + 1e-06)
    value = start * scaling * gain
    return value / (1.0 + jnp.exp(-value))


def residual(start, b2, act_ref, rim_ref, target, first):
    for l in range(3):
        act_ref[l, 0:M1, :] = start[:, lanes(l)]
        target[0:CORE, lanes(l, first)] = strip(act_ref, l, S + 2, 10) + b2[:, lanes(l)]
        target[CORE:M2, lanes(l, first)] = edge(act_ref, l, S + 1, rim_ref.at[27 + l]) + b2[:, lanes(l)]


def activate(start, gain, keep, act_ref, rim_ref, la_ref, le_ref):
    value = jnp.where(keep, silu_of_norm(start, gain), 0.0)
    for l in range(3):
        act_ref[l, 0:M1, :] = value[:, lanes(l)]
        for dx in range(3):
            for y in range(0, 12, 2):
                la_ref[y * WL : (y + 2) * WL, lanes(l, dx * C)] = strip(act_ref, l, y * S + 1 + dx, 2).astype(bf16)
            for dy in range(3):
                rim = edge(act_ref, l, dy * S + dx, rim_ref.at[(dy * 3 + dx) * 3 + l])
                le_ref[:, lanes(l, (dy * 3 + dx) * C)] = rim.astype(bf16)


def taps_of(la_ref, le_ref):
    core = jnp.concatenate([la_ref[dy * WL : dy * WL + CORE, :] for dy in range(3)], axis=1)
    return jnp.concatenate([core, le_ref[...]], axis=0)


def front(
    own_ref, w1_ref, up_ref, w2_hbm, b1_ref, gain_ref, b2_ref, acc_ref, tu_ref, w2_ref,
    t1_ref, sem, x_ref, l1_ref, act_ref, la_ref,
):
    loads = [pltpu.make_async_copy(w2_hbm.at[dt], w2_ref.at[dt], sem.at[dt]) for dt in (2, 0, 1)]
    for load in loads:
        load.start()
    b1, gain, b2 = [ref[...].reshape(1, C) for ref in (b1_ref, gain_ref, b2_ref)]
    taps(w1_ref, t1_ref, 1)
    half = M0 // 2
    packed = own_ref[...].astype(f32)
    x_ref[0:half, :] = packed
    x_ref[half:M0, :] = pltpu.roll(packed, 64, 1)
    x_ref[M0 : M0 + 8, :] = jnp.zeros((8, 128), f32)
    side_by_side(x_ref, 0, l1_ref)
    field = jnp.dot(rows_of(l1_ref, M1), t1_ref[...], preferred_element_type=f32) + b1
    start = field.astype(bf16).astype(f32)
    act_ref[0:M1, :] = start
    kept = act_ref[pl.ds(S + 1, 10 * S), :] + b2
    act_ref[0:M1, :] = jnp.where(inside(M1, 2), silu_of_norm(start, gain), 0.0)
    act_ref[M1 : M1 + 8, :] = jnp.zeros((8, C), f32)
    for dx in range(3):
        la_ref[:, dx * C : (dx + 1) * C] = act_ref[pl.ds(dx, M1), :].astype(bf16)
    groups = (((0,), (1, 2)), ((0, 1), (2,)))
    for py in range(2):
        for px in range(2):
            for ey in range(2):
                for ex in range(2):
                    total = None
                    for dy in groups[py][ey]:
                        for dx in groups[px][ex]:
                            part = up_ref[dy * 3 + dx].astype(f32)
                            total = part if total is None else total + part
                    row = (ey * 2 + ex) * C
                    tu_ref[py * 2 + px, row : row + C, 0:C_UP] = total.T.astype(bf16)
            tu_ref[py * 2 + px, :, C_UP:256] = jnp.zeros((4 * C, 256 - C_UP), bf16)
    loads[0].wait()
    field = kept + jnp.dot(rows_of(la_ref, 10 * S), w2_ref[2], preferred_element_type=f32)
    for l in range(3):
        acc_ref[l, 0 : 10 * S, :] = field[:, lanes(l)]
    for load in loads[1:]:
        load.wait()


def back(
    own_ref, before_ref, older_ref, acc4_ref, w1_ref, tu_ref, w2_ref, b1_ref, gain_ref, b2_ref, bu_ref, out_hbm,
    t1_ref, sem, x_ref, l1_ref, act_ref, rim_ref, la_ref, le_ref, acc_ref, lh_ref, up_ref, out_ref,
):
    b1, gain, b2 = [ref[...].reshape(1, C) for ref in (b1_ref, gain_ref, b2_ref)]
    bu = jnp.concatenate([bu_ref[...].reshape(1, C_UP), jnp.zeros((1, 256 - C_UP), f32)], axis=1)

    half, part = M0 // 2, M0 // 8
    x = lax.axis_index("tm")
    now, before, older = [
        jnp.where(x >= d, ref[...].astype(f32), 0.0) for d, ref in enumerate((own_ref, before_ref, older_ref))
    ]
    lane = place((half, 128), 1)
    for i in range(2):
        past = pltpu.roll(before, 64, 1) if i else before
        old = jnp.concatenate([pltpu.roll(older, 112 - 16 * (4 * i + k), 1) if 4 * i + k < 7 else older for k in range(4)], axis=0)
        x_ref[i * half : (i + 1) * half, :] = jnp.where(
            lane < 48, past, jnp.where(lane < 96, pltpu.roll(now, 112 if i else 48, 1), old)
        )
    x_ref[M0 : M0 + 8, :] = jnp.zeros((8, 128), f32)
    taps(w1_ref, t1_ref, 2)

    rim_ref[...] = jnp.zeros(rim_ref.shape, f32)
    keep = inside(M1, 2)
    for pair in range(2):
        side_by_side(x_ref, (16 - 32 * pair) % 128, l1_ref.at[pair])
        fields = jnp.dot(rows_of(l1_ref.at[pair], M1), t1_ref[...], preferred_element_type=f32)
        for k in range(2):
            frame = 2 * pair + k
            start = (fields[:, k * C : (k + 1) * C] + b1).astype(bf16).astype(f32)
            if pair:
                residual(start, b2, act_ref.at[frame], rim_ref.at[frame], acc_ref, k * C)
            activate(
                start, gain, keep if pair else keep & (x > 0), act_ref.at[frame], rim_ref.at[frame],
                la_ref.at[frame], le_ref.at[frame],
            )
    for l in range(3):
        acc_ref[0:CORE, lanes(l, 2 * C)] = strip(acc4_ref, l, 1, 10)
        acc_ref[CORE:M2, lanes(l, 2 * C)] = edge(acc4_ref, l, 0, rim_ref.at[0, 27 + l])

    for frame in range(4):
        low, high = max(0, frame - 2), min(2, frame)
        weight = jnp.concatenate([w2_ref[frame - t] for t in range(low, high + 1)], axis=1)
        acc_ref[:, low * C : (high + 1) * C] += jnp.dot(
            taps_of(la_ref.at[frame], le_ref.at[frame]), weight, preferred_element_type=f32
        )

    a, b = origin()
    position = place((M2, 1), 0)
    core = position < CORE
    row = jnp.where(core, (position * 2731) >> 16, (position - CORE) >> 1) + a * HL - 1
    column = jnp.where(core, 0, b * WL - 1 + 25 * (position & 1))
    keep = (row >= 0) & (row < GRID * HL) & (column >= 0) & (column < GRID * WL)
    for t in range(3):
        for l in range(3):
            act, rim = act_ref.at[t], rim_ref.at[t]
            field = jnp.where(keep, acc_ref[:, lanes(l, t * C)], 0.0)
            for y in range(10):
                act[l, pl.ds(y * S + 1, WL), :] = field[y * WL : (y + 1) * WL]
            rim[l, 0:EDGES, :] = field[CORE:M2]
            for s in range(2):
                act[l, pl.ds(25 * s, 10, stride=S), :] = rim[l, pl.ds(s, 10, stride=2), :]
            for dx in range(3):
                for y in range(0, 10, 2):
                    lh_ref[t, y * WL : (y + 2) * WL, lanes(l, dx * C)] = strip(act, l, y * S + dx, 2).astype(bf16)
    for py in range(2):
        for px in range(2):
            lhs = jnp.concatenate(
                [
                    jnp.concatenate(
                        [
                            lh_ref[t, (py + ey) * WL : (py + ey) * WL + M3, (px + ex) * C : (px + ex + 1) * C]
                            for t in range(3)
                        ],
                        axis=0,
                    )
                    for ey in range(2)
                    for ex in range(2)
                ],
                axis=1,
            )
            phase = jnp.dot(lhs, tu_ref[py * 2 + px], preferred_element_type=f32) + bu
            for t in range(3):
                for y in range(HL):
                    row = t * M3 + y * WL
                    for side in range(2):
                        up_ref[t, side, 2 * y + py, pl.ds(px, WL, stride=2), :] = phase[
                            row : row + WL, side * 128 : (side + 1) * 128
                        ]
    stores = []
    for t in range(3):
        out_ref[t, 0, :, :, 0:128] = up_ref[t, 0].astype(bf16)
        out_ref[t, 0, :, :, 128:C_UP] = up_ref[t, 1, :, :, 0 : C_UP - 128].astype(bf16)
        stores.append(pltpu.make_async_copy(out_ref.at[t], out_hbm.at[t], sem.at[t]))
        stores[-1].start()
    for store in stores:
        store.wait()


def on_device(
    latent, conv_in_weight, conv_in_bias, first_gain, conv_weight, conv_bias, up_weight, up_bias
):
    w1 = conv_in_weight.reshape(27 * LAT_C, C)
    w2 = pltpu.with_memory_space_constraint(conv_weight.reshape(3, 9 * C, C), pltpu.HBM)
    own, last = pl.pallas_call(
        assemble,
        out_shape=[jax.ShapeDtypeStruct((M0 // 2, 128), bf16), jax.ShapeDtypeStruct((M0 // 8, 128), bf16)],
        in_specs=[VMEM],
        out_specs=[VMEM, VMEM],
        compiler_params=pltpu.CompilerParams(vmem_limit_bytes=8 * 2**20),
        cost_estimate=pl.CostEstimate(flops=10**8, bytes_accessed=10**6, transcendentals=0),
        name="assemble",
    )(gather(latent))
    count = lax.axis_size("tm")
    before = lax.ppermute(own, "tm", [(i, (i + 1) % count) for i in range(count)])
    older = lax.ppermute(last, "tm", [(i, (i + 2) % count) for i in range(count)])
    acc4, tu, w2 = pl.pallas_call(
        front,
        out_shape=[
            jax.ShapeDtypeStruct((3, 16 * S, 128), f32),
            jax.ShapeDtypeStruct((4, 4 * C, 256), bf16),
            pltpu.VMEM((3, 9 * C, C), bf16),
        ],
        in_specs=[VMEM, VMEM, VMEM, HBM, VMEM, VMEM, VMEM],
        out_specs=[VMEM, VMEM, VMEM],
        scratch_shapes=[
            pltpu.VMEM((3 * 256, C), bf16),
            pltpu.SemaphoreType.DMA((3,)),
            pltpu.VMEM((M0 + 8, 128), f32),
            pltpu.VMEM((M0, 256), bf16),
            pltpu.VMEM((M1 + 8, C), f32),
            pltpu.VMEM((M1, 3 * C), bf16),
        ],
        compiler_params=pltpu.CompilerParams(vmem_limit_bytes=24 * 2**20),
        cost_estimate=pl.CostEstimate(flops=10**9, bytes_accessed=10_000_000, transcendentals=10**6),
        name="front",
    )(own, w1, up_weight.transpose(0, 1, 3, 2).reshape(9, C_UP, C), w2, conv_in_bias, first_gain, conv_bias)
    return pl.pallas_call(
        back,
        out_shape=jax.ShapeDtypeStruct((3, 1, 2 * HL, 2 * WL, C_UP), bf16),
        in_specs=[VMEM] * 11,
        out_specs=HBM,
        scratch_shapes=[
            pltpu.VMEM((3 * 256, 2 * C), bf16),
            pltpu.SemaphoreType.DMA((3,)),
            pltpu.VMEM((M0 + 8, 128), f32),
            pltpu.VMEM((2, M0, 256), bf16),
            pltpu.VMEM((4, 3, TALL, 128), f32),
            pltpu.VMEM((4, 30, RIM, 128), f32),
            pltpu.VMEM((4, 12 * WL, 3 * C), bf16),
            pltpu.VMEM((4, EDGES, 9 * C), bf16),
            pltpu.VMEM((M2, 3 * C), f32),
            pltpu.VMEM((3, CORE, 3 * C), bf16),
            pltpu.VMEM((3, 2, 2 * HL, 2 * WL, 128), f32),
            pltpu.VMEM((3, 1, 2 * HL, 2 * WL, C_UP), bf16),
        ],
        compiler_params=pltpu.CompilerParams(vmem_limit_bytes=32 * 2**20),
        cost_estimate=pl.CostEstimate(flops=8 * 10**9, bytes_accessed=12_000_000, transcendentals=10**6),
        name="back",
    )(own, before, older, acc4, w1, tu, w2, conv_in_bias, first_gain, conv_bias, up_bias)


def solution(mesh):
    return jax.shard_map(
        on_device,
        mesh=mesh,
        in_specs=(P("tm", "tile", None), P(), P(), P(), P(), P(), P(), P()),
        out_specs=P("tm", "tile", None, None, None),
        check_vma=False,
    )
```
